32 devices in a mesh: pool: 2 (over core), pb: 4 (over z), ka: 4 (over y, x).
Axes of the slice: x: 2, y: 2, z: 4, core: 2. Of those that a mesh axis runs over, the one named last changes fastest.
Arguments:
- tokens: bfloat16 [2048, 5376], P(('pb', 'ka'), 'pool'), may hold values from -6 to 6
- modality: int32 [2048], P('pb'), may hold values from 0 to 1, as said below
- proj_weight: bfloat16 [2, 5376, 2048], P('pool', None, 'ka'), may hold values from -0.078125 to 0.078125
- out_grad: bfloat16 [2, 2048, 512], P('pool', 'pb', 'ka'), may hold values from -24 to 24
Outputs:
- grad_tokens: bfloat16 [2048, 5376], P(('pb', 'ka'), 'pool')
- grad_weight: float32 [2, 5376, 2048], P('pool', 'pb', 'ka')
The draws below stay inside these ranges and needn't reach their ends.
Inputs may be any that keep to these rules, and one draw needn't show every extreme that they name: `modality`: 1 marks image tokens; they stand in runs whose lengths are multiples of 256 except at the sequence's start and end, and both kinds occur.
All inputs are finite; a program needn't handle non-finite values.
Results may differ from the reference program's by a relative error of at most 0.018.
Values may be sent and summed in bfloat16 or wider, within the bound.
A program may use at most 192 MiB of HBM per device.

```python
import math
import jax
import jax.numpy as jnp
from jax import lax

D = 5376
HD = 128
QPK = 2
IMG = 256
KV = 4
S = 2048
PW = 2048
N_PB = 4


def draw_modality(key, part):
    first_key, second_key = jax.random.split(jax.random.fold_in(key, 7))
    offset = jax.random.randint(first_key, (), 0, IMG)
    span_total = S // IMG + 2
    span_kinds = jax.random.randint(second_key, (span_total,), 0, 2)
    span_kinds = span_kinds.at[0].set(1).at[1].set(0)
    span_index = (jnp.arange(S, dtype=jnp.int32) + offset) // IMG
    return span_kinds[span_index].astype(jnp.int32)


def spiked(result, key, source, target, parts, factor):
    def block_of(position):
        return (jnp.arange(result.shape[position]) // (result.shape[position] // parts)).reshape((-1,) + (1,) * (result.ndim - 1 - position))

    first = jax.random.permutation(key, parts)[block_of(target)]
    second = (block_of(target) + parts // 2) % parts
    return jnp.where((block_of(source) == first) | (block_of(source) == second), factor * result, result)


def block_levels(stream_key, extent, pieces, smallest, largest):
    level = 1.0
    for position, shards_of in pieces:
        heights = jax.random.uniform(jax.random.fold_in(jax.random.fold_in(stream_key, 6), position), (shards_of,), jnp.float32, smallest / len(pieces), largest / len(pieces))
        level = level * jnp.repeat(jnp.exp(heights), extent[position] // shards_of).reshape((-1,) + (1,) * (len(extent) - 1 - position))
    return level


def noise(key, shape, width, most, cuts=(), kind=jnp.bfloat16):
    factor_of = block_levels(key, shape, cuts, -0.22, 0.18) if cuts else 1.0
    result = jax.random.normal(key, shape, jnp.float32) * width * factor_of
    return jnp.minimum(jnp.maximum(result, -most), most).astype(kind)


def heavy_noise(rng, extent, spread, reach, cuts, heavy, kind=jnp.bfloat16):
    drawn = spread * jax.random.normal(rng, extent, jnp.float32)
    if cuts:
        drawn = drawn * block_levels(rng, extent, cuts, -0.22, 0.18)
    return jnp.clip(spiked(drawn, jax.random.fold_in(rng, 3), *heavy), -reach, reach).astype(kind)


def setup_inputs(seed: int = 0) -> dict:
    arg_keys = jax.random.split(jax.random.key(seed), 5)
    return {
        "tokens": heavy_noise(arg_keys[0], (S, D), 1.0, 6.0, ((0, 16), (1, 2)), (0, 1, 16, 2.0)),
        "modality": draw_modality(jax.random.fold_in(arg_keys[4], 71), 0),
        "proj_weight": noise(arg_keys[2], (2, D, PW), D ** -0.5, 0.078125, ((0, 2), (2, 4))),
        "out_grad": noise(arg_keys[3], (QPK, S, KV * HD), 4.0, 24.0, ((0, 2), (1, 4), (2, 4))),
    }


def make_advance(key_rows, value_rows, scaling):
    contract_one = (((1,), (1,)), ((), ()))
    contract_zero = (((0,), (0,)), ((), ()))

    def advance(running, block_in):
        q_block, o_block = block_in
        scores = lax.dot_general(q_block, key_rows, contract_one, preferred_element_type=jnp.float32) * scaling
        row_max = lax.optimization_barrier(jnp.max(scores, axis=1, keepdims=True))
        log_total = row_max + jnp.log(lax.optimization_barrier(jnp.sum(jnp.exp(scores - row_max), axis=1, keepdims=True)))
        softmax = jnp.exp(scores - log_total)
        grad_prob = lax.dot_general(o_block, value_rows, contract_one, preferred_element_type=jnp.float32)
        delta = lax.optimization_barrier(jnp.sum(softmax * grad_prob, axis=1, keepdims=True))
        grad_score = (softmax * (grad_prob - delta)).astype(jnp.bfloat16)
        grad_query = jnp.dot(grad_score, key_rows, preferred_element_type=jnp.float32) * scaling
        key_part = lax.dot_general(grad_score, q_block, contract_zero, preferred_element_type=jnp.float32) * scaling
        value_part = lax.dot_general(softmax.astype(jnp.bfloat16), o_block, contract_zero, preferred_element_type=jnp.float32)
        key_low = lax.optimization_barrier(key_part.astype(jnp.bfloat16)).astype(jnp.float32)
        value_low = lax.optimization_barrier(value_part.astype(jnp.bfloat16)).astype(jnp.float32)
        return ((running[0] + key_low, running[1] + value_low), grad_query)
    return advance

def reference(tokens, modality, proj_weight, out_grad):
    scaling = 1.0 / math.sqrt(HD)
    group_width = (QPK + 2) * HD
    contract_one = (((1,), (1,)), ((), ()))
    contract_zero = (((0,), (0,)), ((), ()))
    is_image = (modality == 1)[:, None]
    text_proj = jnp.dot(tokens, proj_weight[0], preferred_element_type=jnp.float32)
    image_proj = jnp.dot(tokens, proj_weight[1], preferred_element_type=jnp.float32)
    projected = jnp.where(is_image, image_proj, text_proj).astype(jnp.bfloat16)
    block_rows = S // N_PB
    group_parts = []
    for group in range(KV):
        base = group * group_width
        key_rows = projected[:, base + QPK * HD:base + (QPK + 1) * HD]
        value_rows = projected[:, base + (QPK + 1) * HD:base + group_width]
        advance = make_advance(key_rows, value_rows, scaling)
        grad_keys = jnp.zeros((S, HD), jnp.float32)
        grad_values = jnp.zeros((S, HD), jnp.float32)
        head_grads = []
        for within in range(QPK):
            queries = projected[:, base + within * HD:base + (within + 1) * HD].reshape(N_PB, block_rows, HD)
            cotangent = out_grad[within, :, group * HD:(group + 1) * HD].reshape(N_PB, block_rows, HD)
            (grad_keys, grad_values), grad_query = lax.scan(advance, (grad_keys, grad_values), (queries, cotangent))
            head_grads.append(grad_query.reshape(S, HD))
        group_parts.append(jnp.concatenate(head_grads + [grad_keys, grad_values], axis=1))
    grad_proj = jnp.concatenate(group_parts, axis=1).astype(jnp.bfloat16)
    back_sum = jnp.zeros((S, D), jnp.float32)
    for group in range(KV):
        base = group * group_width
        grad_cols = grad_proj[:, base:base + group_width]
        back_text = lax.dot_general(grad_cols, proj_weight[0][:, base:base + group_width], contract_one, preferred_element_type=jnp.float32)
        back_image = lax.dot_general(grad_cols, proj_weight[1][:, base:base + group_width], contract_one, preferred_element_type=jnp.float32)
        chosen = jnp.where(is_image, back_image, back_text)
        back_sum = back_sum + lax.optimization_barrier(chosen.astype(jnp.bfloat16)).astype(jnp.float32)
    grad_tokens = back_sum.astype(jnp.bfloat16)
    text_part = jnp.where(is_image, jnp.zeros_like(grad_proj), grad_proj)
    image_part = jnp.where(is_image, grad_proj, jnp.zeros_like(grad_proj))
    text_weight = lax.dot_general(tokens, text_part, contract_zero, preferred_element_type=jnp.float32)
    image_weight = lax.dot_general(tokens, image_part, contract_zero, preferred_element_type=jnp.float32)
    grad_weight = jnp.stack([text_weight, image_weight])
    return (grad_tokens, grad_weight)
```

```python
import functools
import math

import jax
import jax.numpy as jnp
from jax import lax
from jax.experimental import pallas as pl
from jax.experimental.pallas import tpu as pltpu
from jax.sharding import PartitionSpec as P


def plain_shards(tokens, modality, proj_weight, out_grad):
    contract_one = (((1,), (1,)), ((), ()))
    contract_zero = (((0,), (0,)), ((), ()))
    pool_index = lax.axis_index("pool")
    pool_count = lax.axis_size("pool")
    head_size = out_grad.shape[2]
    scaling = 1.0 / math.sqrt(head_size)
    token_count = tokens.shape[0]
    half_width = tokens.shape[1]
    group_width = proj_weight.shape[2]
    weight = proj_weight[0].reshape(pool_count, half_width, group_width)
    gathered = lax.all_gather(tokens[None], ("pool", "ka"), axis=0, tiled=True)
    query_count = gathered.shape[0] // pool_count * token_count
    block_tokens = gathered.reshape(pool_count, query_count, half_width)
    owned = (modality == pool_index)[:, None]
    local_proj = jnp.where(
        owned,
        lax.dot_general(
            block_tokens, weight, (((0, 2), (0, 1)), ((), ())), preferred_element_type=jnp.float32
        ),
        0.0,
    )
    projected = lax.psum(local_proj.astype(jnp.bfloat16), "pool")
    queries = lax.dynamic_slice_in_dim(projected, pool_index * head_size, head_size, 1)
    half_rows = query_count // pool_count
    own_keys = projected[:, group_width - 2 * head_size :].reshape(
        pool_count, half_rows, 2 * head_size
    )
    key_value = lax.all_gather(own_keys, "pb", axis=1, tiled=True).reshape(-1, 2 * head_size)
    key_rows = key_value[:, :head_size]
    value_rows = key_value[:, head_size:]
    cotangent = out_grad[0]
    tile_rows = min(512, query_count)
    tile_count = query_count // tile_rows
    q_tiles = queries.reshape(tile_count, tile_rows, head_size)
    o_tiles = cotangent.reshape(tile_count, tile_rows, head_size)

    def advance(running, tile_in):
        q_tile, o_tile = tile_in
        scores = (
            lax.dot_general(q_tile, key_rows, contract_one, preferred_element_type=jnp.float32)
            * scaling
        )
        row_max = jnp.max(scores, axis=1, keepdims=True)
        log_total = row_max + jnp.log(jnp.sum(jnp.exp(scores - row_max), axis=1, keepdims=True))
        softmax = jnp.exp(scores - log_total)
        grad_prob = lax.dot_general(
            o_tile, value_rows, contract_one, preferred_element_type=jnp.float32
        )
        delta = jnp.sum(softmax * grad_prob, axis=1, keepdims=True)
        grad_score = (softmax * (grad_prob - delta)).astype(jnp.bfloat16)
        grad_query = jnp.dot(grad_score, key_rows, preferred_element_type=jnp.float32) * scaling
        new_keys = (
            running[0]
            + lax.dot_general(grad_score, q_tile, contract_zero, preferred_element_type=jnp.float32)
            * scaling
        )
        new_values = running[1] + lax.dot_general(
            softmax.astype(jnp.bfloat16), o_tile, contract_zero, preferred_element_type=jnp.float32
        )
        return ((new_keys, new_values), grad_query)

    key_count = key_rows.shape[0]
    start_state = (
        jnp.zeros((key_count, head_size), jnp.float32),
        jnp.zeros((key_count, head_size), jnp.float32),
    )
    (grad_keys, grad_values), grad_query = lax.scan(advance, start_state, (q_tiles, o_tiles))
    key_terms = jnp.concatenate([grad_keys, grad_values], axis=1)
    key_cell = lax.psum_scatter(
        key_terms.astype(jnp.bfloat16), ("pool", "pb"), scatter_dimension=0, tiled=True
    )
    query_low = grad_query.reshape(query_count, head_size).astype(jnp.bfloat16)
    both_queries, key_block = (
        lax.all_gather(query_low, "pool", axis=1, tiled=True),
        lax.all_gather(key_cell, "pool", axis=0, tiled=True),
    )
    grad_proj = jnp.concatenate([both_queries, key_block], axis=1)
    masked = jnp.where(owned, grad_proj, jnp.zeros_like(grad_proj))
    back = jnp.einsum("rj,pcj->prc", masked, weight, preferred_element_type=jnp.float32)
    stacked = back.reshape(pool_count * (query_count // token_count), token_count, half_width)
    token_sum = lax.psum_scatter(
        stacked.astype(jnp.bfloat16), ("pool", "ka"), scatter_dimension=0, tiled=True
    ).astype(jnp.float32)[0]
    grad_tokens = token_sum.astype(jnp.bfloat16)
    term = jnp.einsum(
        "prc,rj->pcj", block_tokens, masked, preferred_element_type=jnp.float32
    ).reshape(-1, group_width)
    grad_weight = lax.psum_scatter(
        term.astype(jnp.bfloat16), "pb", scatter_dimension=0, tiled=True
    ).astype(jnp.float32)
    return (grad_tokens, grad_weight[None])


BF16 = jnp.bfloat16
F32 = jnp.float32
NT = (((1,), (1,)), ((), ()))


def divisor(total, unit, most):
    best = unit
    for size in range(unit, most + 1, unit):
        if total % size == 0:
            best = size
    return best


def fused(
    dims, tok, xt, mod, weight_hbm, cot, out_tok, out_weight,
    tokbuf, wbuf, xtbuf, modbuf, projloc, projrecv, qbuf, kvbuf, ktbuf, dkacc, dvacc,
    dkv, dkvp, dkvs, dkvr, gp, mgp, bsend, brecv, bsum, kar, load_sem, ss, rs,
):
    n_pb, n_ka, rows, half, group, hd, q_rows, offsets = dims
    scaling = 1.0 / math.sqrt(hd)
    p, b, k = lax.axis_index("pool"), lax.axis_index("pb"), lax.axis_index("ka")
    other = 1 - p
    q_half = q_rows // 2
    hp = n_pb // 2
    n_c, chunk = bsend.shape[0], bsend.shape[2]
    slice_rows = xt.shape[1]
    kv_at = group - 2 * hd
    partner = (other, b, k)
    sends = []

    def pb_dev(d):
        return (p, lax.rem(b + d, n_pb), k)

    def ka_dev(d):
        return (p, b, lax.rem(k + d, n_ka))

    def b_from(d):
        return lax.rem(b - d + n_pb, n_pb)

    def k_from(d):
        return lax.rem(k - d + n_ka, n_ka)

    def remote(src, dst, name, i, dev):
        at = offsets[name] + i
        return pltpu.make_async_remote_copy(
            src_ref=src, dst_ref=dst, send_sem=ss.at[at], recv_sem=rs.at[at],
            device_id=dev, device_id_type=pl.DeviceIdType.MESH,
        )

    def send(src, dst, name, i, dev):
        copy = remote(src, dst, name, i, dev)
        copy.start()
        sends.append(copy)

    def arrived(dst, name, i):
        remote(dst, dst, name, i, partner).wait_recv()

    def ka_rows(index):
        return pl.ds(pl.multiple_of(index * rows, rows), rows)

    barrier = pltpu.get_barrier_semaphore()
    devs = [partner] + [pb_dev(d) for d in range(1, n_pb)] + [ka_dev(d) for d in range(1, n_ka)]
    for dev in devs:
        pl.semaphore_signal(barrier, inc=1, device_id=dev, device_id_type=pl.DeviceIdType.MESH)
    load = pltpu.make_async_copy(weight_hbm.at[0], wbuf, load_sem)
    load.start()
    pl.semaphore_wait(barrier, len(devs))

    for d in range(1, n_ka):
        send(tok, tokbuf.at[p, ka_rows(k)], "tok_ka", d, ka_dev(d))
    send(tok, tokbuf.at[p, ka_rows(k)], "tok_fw", 0, partner)
    for d in range(1, n_pb):
        send(mod, modbuf.at[b], "mod", d, pb_dev(d))

    mine = lax.div(b, hp) == p
    for d in range(1, n_pb):
        target = lax.rem(b + d, n_pb)

        @pl.when(lax.div(target, hp) == p)
        def _(d=d, target=target):
            remote(
                xt.at[lax.rem(target, hp)], xtbuf.at[b, :, ka_rows(k)], "xt_z", d, pb_dev(d)
            ).start()

    tokbuf[p, ka_rows(k), :] = tok[...]
    modbuf[b] = mod[...]

    @pl.when(mine)
    def _():
        xtbuf[b, :, ka_rows(k)] = xt[lax.rem(b, hp)]

    for d in range(1, n_ka):
        region = tokbuf.at[p, ka_rows(k_from(d))]
        arrived(region, "tok_ka", d)
        send(region, region, "tok_fw", d, partner)
    for d in range(n_ka):
        arrived(tokbuf.at[other, ka_rows(k_from(d))], "tok_fw", d)
    load.wait()

    def own_mask(index):
        return modbuf[index].astype(F32)[:, :1] == p.astype(F32)

    proj = jnp.dot(tokbuf[0], wbuf[:half], preferred_element_type=F32)
    proj += jnp.dot(tokbuf[1], wbuf[half:], preferred_element_type=F32)
    projloc[...] = proj.astype(BF16)
    send(projloc, projrecv, "pj", 0, partner)

    @pl.when(mine)
    def _():
        for d in range(1, n_pb):
            arrived(xtbuf.at[b_from(d), :, ka_rows(k)], "xt_z", d)
        for d in range(1, n_ka):
            region = xtbuf.at[:, :, ka_rows(k)]
            remote(region, region, "xt_ka", d, ka_dev(d)).start()
        region = xtbuf.at[:, :, ka_rows(k)]
        remote(region, region, "xt_fw", 0, partner).start()

    arrived(projrecv, "pj", 0)
    projected = jnp.where(own_mask(b), projloc[...].astype(F32), projrecv[...].astype(F32)).astype(BF16)
    qbuf[...] = jnp.where(p == 0, projected[:, :hd].astype(F32), projected[:, hd : 2 * hd].astype(F32)).astype(BF16)
    kvbuf[b] = projected[:, kv_at:].reshape(2, q_half, 2 * hd)
    for d in range(1, n_pb):
        send(kvbuf.at[b, p], kvbuf.at[b, p], "kv_z", d, pb_dev(d))
    for d in range(1, n_pb):
        region = kvbuf.at[b_from(d), p]
        arrived(region, "kv_z", d)
        send(region, region, "kv_fw", d, partner)
    for d in range(1, n_pb):
        arrived(kvbuf.at[b_from(d), other], "kv_fw", d)

    keys = n_pb * q_rows
    ktbuf[...] = jnp.transpose(
        kvbuf[:, :, :, :hd].reshape(keys, hd).astype(F32)
    ).astype(BF16)
    dkacc[...] = jnp.zeros_like(dkacc)
    dvacc[...] = jnp.zeros_like(dvacc)
    tile = min(256, q_rows)

    def attend(t, carry):
        at = pl.ds(pl.multiple_of(t * tile, tile), tile)
        q = qbuf[at, :]
        o = cot[0, at, :]
        key_rows = kvbuf[:, :, :, :hd].reshape(keys, hd)
        value_rows = kvbuf[:, :, :, hd:].reshape(keys, hd)
        scores = lax.dot_general(key_rows, q, NT, preferred_element_type=F32) * scaling
        high = jnp.max(scores, axis=0, keepdims=True)
        raised = jnp.exp(scores - high)
        softmax = raised * (1.0 / jnp.sum(raised, axis=0, keepdims=True))
        grad_prob = lax.dot_general(value_rows, o, NT, preferred_element_type=F32)
        delta = jnp.sum(softmax * grad_prob, axis=0, keepdims=True)
        grad_score = (softmax * (grad_prob - delta)).astype(BF16)
        dkacc[...] += jnp.dot(grad_score, q, preferred_element_type=F32)
        dvacc[...] += jnp.dot(softmax.astype(BF16), o, preferred_element_type=F32)
        dq = jnp.dot(ktbuf[...], grad_score, preferred_element_type=F32) * scaling
        dq = jnp.transpose(dq).astype(BF16)

        @pl.when(p == 0)
        def _():
            gp[b, at, :hd] = dq

        @pl.when(p == 1)
        def _():
            gp[b, at, hd : 2 * hd] = dq

        return carry

    lax.fori_loop(0, q_rows // tile, attend, 0)
    dkv[:, :, :, :hd] = (dkacc[...] * scaling).astype(BF16).reshape(n_pb, 2, q_half, hd)
    dkv[:, :, :, hd:] = dvacc[...].astype(BF16).reshape(n_pb, 2, q_half, hd)
    send(dkv.at[:, other], dkvp, "dk_p", 0, partner)
    arrived(dkvp, "dk_p", 0)
    dkvs[...] = (dkv[:, p].astype(F32) + dkvp[...].astype(F32)).astype(BF16)
    for d in range(1, n_pb):
        send(dkvs.at[lax.rem(b + d, n_pb)], dkvr.at[d], "dk_z", d, pb_dev(d))

    def q_cols(pool):
        return pl.ds(pl.multiple_of(pool * hd, hd), hd)

    def half_rows(pool):
        return pl.ds(pl.multiple_of(pool * q_half, q_half), q_half)

    dq_own = gp.at[b, :, q_cols(p)]
    send(dq_own, dq_own, "dq_p", 0, partner)
    for d in range(1, n_pb):
        send(dq_own, dq_own, "dq_z", d, pb_dev(d))

    @pl.when(mine)
    def _():
        for d in range(1, n_ka):
            region = xtbuf.at[:, :, ka_rows(k_from(d))]
            arrived(region, "xt_ka", d)
            remote(region, region, "xt_fw", d, partner).start()

    total = dkvs[b].astype(F32)
    for d in range(1, n_pb):
        arrived(dkvr.at[d], "dk_z", d)
        total += dkvr[d].astype(F32)
    gp[b, half_rows(p), kv_at:] = total.astype(BF16)
    kv_own = gp.at[b, half_rows(p), pl.ds(kv_at, 2 * hd)]
    send(kv_own, kv_own, "gk_p", 0, partner)
    for d in range(1, n_pb):
        send(kv_own, kv_own, "gk_z", d, pb_dev(d))
    arrived(gp.at[b, :, q_cols(other)], "dq_p", 0)
    arrived(gp.at[b, half_rows(other), pl.ds(kv_at, 2 * hd)], "gk_p", 0)

    mgp[b] = jnp.where(own_mask(b), gp[b].astype(F32), 0.0).astype(BF16)

    def back_chunk(c, carry):
        def product(pool):
            at = pl.ds(pl.multiple_of(pool * half + c * chunk, 128), chunk)
            return lax.dot_general(mgp[b], wbuf[at, :], NT, preferred_element_type=F32)

        bsend[c] = product(other).astype(BF16)
        remote(bsend.at[c], brecv.at[c], "bk_p", c, partner).start()
        own = product(p).astype(BF16).astype(F32)
        arrived(brecv.at[c], "bk_p", c)
        bsum[c] = (own + brecv[c].astype(F32)).astype(BF16)
        for d in range(1, n_ka):
            remote(
                bsum.at[c, ka_rows(lax.rem(k + d, n_ka))], kar.at[d, c],
                "bk_ka", d * n_c + c, ka_dev(d),
            ).start()
        return carry

    lax.fori_loop(0, n_c, back_chunk, 0)

    for d in range(1, n_pb):
        region = gp.at[b_from(d), :, q_cols(p)]
        arrived(region, "dq_z", d)
        send(region, region, "dq_p", d, partner)
    for d in range(1, n_pb):
        region = gp.at[b_from(d), half_rows(p), pl.ds(kv_at, 2 * hd)]
        arrived(region, "gk_z", d)
        send(region, region, "gk_p", d, partner)
    for d in range(1, n_pb):
        arrived(modbuf.at[b_from(d)], "mod", d)
    for d in range(1, n_pb):
        arrived(gp.at[b_from(d), :, q_cols(other)], "dq_p", d)
        arrived(gp.at[b_from(d), half_rows(other), pl.ds(kv_at, 2 * hd)], "gk_p", d)
        source = b_from(d)
        mgp[source] = jnp.where(own_mask(source), gp[source].astype(F32), 0.0).astype(BF16)

    @pl.when(jnp.logical_not(mine))
    def _():
        for d in range(n_ka):
            arrived(xtbuf.at[:, :, ka_rows(k_from(d))], "xt_fw", d)

    w_tile = divisor(slice_rows, 16, 512)

    def weight_rows(t, carry):
        at = pl.ds(pl.multiple_of(t * w_tile, 16), w_tile)
        acc = jnp.dot(xtbuf[0, at, :], mgp[0], preferred_element_type=F32)
        for i in range(1, n_pb):
            acc += jnp.dot(xtbuf[i, at, :], mgp[i], preferred_element_type=F32)
        out_weight[0, at, :] = acc
        return carry

    lax.fori_loop(0, slice_rows // w_tile, weight_rows, 0)

    for c in range(n_c):
        acc = bsum[c, ka_rows(k), :].astype(F32)
        for d in range(1, n_ka):
            arrived(kar.at[d, c], "bk_ka", d * n_c + c)
            acc += kar[d, c].astype(F32)
        out_tok[:, c * chunk : (c + 1) * chunk] = acc.astype(BF16)

    for copy in sends:
        copy.wait_send()
    for d in range(1, n_pb):
        target = lax.rem(b + d, n_pb)

        @pl.when(lax.div(target, hp) == p)
        def _(d=d):
            remote(xt.at[0], xtbuf.at[b, :, ka_rows(k)], "xt_z", d, pb_dev(d)).wait_send()

    @pl.when(mine)
    def _():
        region = xtbuf.at[:, :, ka_rows(k)]
        for d in range(1, n_ka):
            remote(region, region, "xt_ka", d, ka_dev(d)).wait_send()
        for d in range(n_ka):
            region = xtbuf.at[:, :, ka_rows(k_from(d))]
            remote(region, region, "xt_fw", d, partner).wait_send()

    def sent(c, carry):
        remote(bsend.at[c], brecv.at[c], "bk_p", c, partner).wait_send()
        for d in range(1, n_ka):
            remote(
                bsum.at[c, ka_rows(lax.rem(k + d, n_ka))], kar.at[d, c],
                "bk_ka", d * n_c + c, ka_dev(d),
            ).wait_send()
        return carry

    lax.fori_loop(0, n_c, sent, 0)


def shards(tokens, modality, proj_weight, out_grad):
    n_pool, n_pb, n_ka = (lax.axis_size(name) for name in ("pool", "pb", "ka"))
    rows, half = tokens.shape
    group = proj_weight.shape[2]
    width = proj_weight.shape[1]
    q_rows, hd = out_grad.shape[1:]
    keys = n_pb * q_rows
    slice_rows = width // n_pb
    chunk = divisor(half, 128, 512)
    n_c = half // chunk
    vmem, scratch_bytes = [], 0
    shapes = [
        ((2, q_rows, half), BF16), ((width, group), BF16), ((n_pb, slice_rows, q_rows), BF16),
        ((n_pb, q_rows, hd), BF16), ((q_rows, group), BF16), ((q_rows, group), BF16),
        ((q_rows, hd), BF16), ((n_pb, 2, q_rows // 2, 2 * hd), BF16), ((hd, keys), BF16),
        ((keys, hd), F32), ((keys, hd), F32), ((n_pb, 2, q_rows // 2, 2 * hd), BF16),
        ((n_pb, q_rows // 2, 2 * hd), BF16), ((n_pb, q_rows // 2, 2 * hd), BF16),
        ((n_pb, q_rows // 2, 2 * hd), BF16), ((n_pb, q_rows, group), BF16),
        ((n_pb, q_rows, group), BF16), ((n_c, q_rows, chunk), BF16), ((n_c, q_rows, chunk), BF16),
        ((n_c, q_rows, chunk), BF16), ((n_ka, n_c, rows, chunk), BF16),
    ]
    for shape, kind in shapes:
        vmem.append(pltpu.VMEM(shape, kind))
        scratch_bytes += math.prod(shape) * jnp.dtype(kind).itemsize
    scratch_bytes += 5 * keys * min(256, q_rows) * 4 + slice_rows * group * 4
    if scratch_bytes > 58 * 2**20 or n_pool != 2 or n_pb % 2:
        return plain_shards(tokens, modality, proj_weight, out_grad)
    offsets, count = {}, 0
    for name, size in (
        ("tok_ka", n_ka), ("tok_fw", n_ka), ("mod", n_pb), ("xt_z", n_pb), ("xt_ka", n_ka),
        ("xt_fw", n_ka), ("pj", 1), ("kv_z", n_pb), ("kv_fw", n_pb), ("dk_p", 1), ("dk_z", n_pb),
        ("dq_p", n_pb), ("dq_z", n_pb), ("gk_p", n_pb), ("gk_z", n_pb), ("bk_p", n_c),
        ("bk_ka", n_ka * n_c),
    ):
        offsets[name] = count
        count += size
    dims = (n_pb, n_ka, rows, half, group, hd, q_rows, offsets)
    in_vmem = pl.BlockSpec(memory_space=pltpu.VMEM)
    turned = tokens.T.reshape(n_pb // 2, slice_rows, rows)
    kinds = jnp.broadcast_to(modality.astype(BF16)[:, None], (q_rows, hd))
    return pl.pallas_call(
        functools.partial(fused, dims),
        out_shape=(
            jax.ShapeDtypeStruct((rows, half), BF16),
            jax.ShapeDtypeStruct((1, slice_rows, group), F32),
        ),
        in_specs=[in_vmem, in_vmem, in_vmem, pl.BlockSpec(memory_space=pl.ANY), in_vmem],
        out_specs=(in_vmem, in_vmem),
        scratch_shapes=vmem
        + [
            pltpu.SemaphoreType.DMA,
            pltpu.SemaphoreType.DMA((count,)),
            pltpu.SemaphoreType.DMA((count,)),
        ],
        compiler_params=pltpu.CompilerParams(
            collective_id=0, has_side_effects=True, vmem_limit_bytes=62 * 2**20
        ),
    )(tokens, turned, kinds, proj_weight, out_grad)


def solution(mesh):
    return jax.shard_map(
        shards,
        mesh=mesh,
        in_specs=(P(("pb", "ka"), "pool"), P("pb"), P("pool", None, "ka"), P("pool", "pb", "ka")),
        out_specs=(P(("pb", "ka"), "pool"), P("pool", "pb", "ka")),
        check_vma=False,
    )
```

```python
import functools
import math

import jax
import jax.numpy as jnp
from jax import lax
from jax.experimental import pallas as pl
from jax.experimental.pallas import tpu as pltpu
from jax.sharding import PartitionSpec as P


def plain_shards(tokens, modality, proj_weight, out_grad):
    contract_one = (((1,), (1,)), ((), ()))
    contract_zero = (((0,), (0,)), ((), ()))
    pool_index = lax.axis_index("pool")
    pool_count = lax.axis_size("pool")
    head_size = out_grad.shape[2]
    scaling = 1.0 / math.sqrt(head_size)
    token_count = tokens.shape[0]
    half_width = tokens.shape[1]
    group_width = proj_weight.shape[2]
    weight = proj_weight[0].reshape(pool_count, half_width, group_width)
    gathered = lax.all_gather(tokens[None], ("pool", "ka"), axis=0, tiled=True)
    query_count = gathered.shape[0] // pool_count * token_count
    block_tokens = gathered.reshape(pool_count, query_count, half_width)
    owned = (modality == pool_index)[:, None]
    local_proj = jnp.where(
        owned,
        lax.dot_general(
            block_tokens, weight, (((0, 2), (0, 1)), ((), ())), preferred_element_type=jnp.float32
        ),
        0.0,
    )
    projected = lax.psum(local_proj.astype(jnp.bfloat16), "pool")
    queries = lax.dynamic_slice_in_dim(projected, pool_index * head_size, head_size, 1)
    half_rows = query_count // pool_count
    own_keys = projected[:, group_width - 2 * head_size :].reshape(
        pool_count, half_rows, 2 * head_size
    )
    key_value = lax.all_gather(own_keys, "pb", axis=1, tiled=True).reshape(-1, 2 * head_size)
    key_rows = key_value[:, :head_size]
    value_rows = key_value[:, head_size:]
    cotangent = out_grad[0]
    tile_rows = min(512, query_count)
    tile_count = query_count // tile_rows
    q_tiles = queries.reshape(tile_count, tile_rows, head_size)
    o_tiles = cotangent.reshape(tile_count, tile_rows, head_size)

    def advance(running, tile_in):
        q_tile, o_tile = tile_in
        scores = (
            lax.dot_general(q_tile, key_rows, contract_one, preferred_element_type=jnp.float32)
            * scaling
        )
        row_max = jnp.max(scores, axis=1, keepdims=True)
        log_total = row_max + jnp.log(jnp.sum(jnp.exp(scores - row_max), axis=1, keepdims=True))
        softmax = jnp.exp(scores - log_total)
        grad_prob = lax.dot_general(
            o_tile, value_rows, contract_one, preferred_element_type=jnp.float32
        )
        delta = jnp.sum(softmax * grad_prob, axis=1, keepdims=True)
        grad_score = (softmax * (grad_prob - delta)).astype(jnp.bfloat16)
        grad_query = jnp.dot(grad_score, key_rows, preferred_element_type=jnp.float32) * scaling
        new_keys = (
            running[0]
            + lax.dot_general(grad_score, q_tile, contract_zero, preferred_element_type=jnp.float32)
            * scaling
        )
        new_values = running[1] + lax.dot_general(
            softmax.astype(jnp.bfloat16), o_tile, contract_zero, preferred_element_type=jnp.float32
        )
        return ((new_keys, new_values), grad_query)

    key_count = key_rows.shape[0]
    start_state = (
        jnp.zeros((key_count, head_size), jnp.float32),
        jnp.zeros((key_count, head_size), jnp.float32),
    )
    (grad_keys, grad_values), grad_query = lax.scan(advance, start_state, (q_tiles, o_tiles))
    key_terms = jnp.concatenate([grad_keys, grad_values], axis=1)
    key_cell = lax.psum_scatter(
        key_terms.astype(jnp.bfloat16), ("pool", "pb"), scatter_dimension=0, tiled=True
    )
    query_low = grad_query.reshape(query_count, head_size).astype(jnp.bfloat16)
    both_queries, key_block = (
        lax.all_gather(query_low, "pool", axis=1, tiled=True),
        lax.all_gather(key_cell, "pool", axis=0, tiled=True),
    )
    grad_proj = jnp.concatenate([both_queries, key_block], axis=1)
    masked = jnp.where(owned, grad_proj, jnp.zeros_like(grad_proj))
    back = jnp.einsum("rj,pcj->prc", masked, weight, preferred_element_type=jnp.float32)
    stacked = back.reshape(pool_count * (query_count // token_count), token_count, half_width)
    token_sum = lax.psum_scatter(
        stacked.astype(jnp.bfloat16), ("pool", "ka"), scatter_dimension=0, tiled=True
    ).astype(jnp.float32)[0]
    grad_tokens = token_sum.astype(jnp.bfloat16)
    term = jnp.einsum(
        "prc,rj->pcj", block_tokens, masked, preferred_element_type=jnp.float32
    ).reshape(-1, group_width)
    grad_weight = lax.psum_scatter(
        term.astype(jnp.bfloat16), "pb", scatter_dimension=0, tiled=True
    ).astype(jnp.float32)
    return (grad_tokens, grad_weight[None])


BF16 = jnp.bfloat16
F32 = jnp.float32
NT = (((1,), (1,)), ((), ()))


def divisor(total, unit, most):
    best = unit
    for size in range(unit, most + 1, unit):
        if total % size == 0:
            best = size
    return best


def fused(
    dims, tok, mod, weight_hbm, cot, out_tok, out_weight,
    tokbuf, wbuf, xtbuf, modbuf, projloc, projrecv, qbuf, kvbuf, ktbuf, prob, score,
    dkv, dkvp, dkvs, dkvr, gp, mgp, bsend, brecv, bsum, kar, rel, xt, wout, load_sem, store_sem, ss, rs,
):
    n_pb, n_ka, rows, half, group, hd, q_rows, offsets = dims
    scaling = 1.0 / math.sqrt(hd)
    p, b, k = lax.axis_index("pool"), lax.axis_index("pb"), lax.axis_index("ka")
    other = 1 - p
    q_half = q_rows // 2
    hp = n_pb // 2
    n_c, chunk = bsend.shape[0], bsend.shape[2]
    slice_rows = xtbuf.shape[1]
    part = rows // 2
    low, high_bit = lax.rem(k, 2), lax.div(k, 2)
    near = [
        k,
        2 * high_bit + 1 - low,
        2 * (1 - high_bit) + low,
        2 * (1 - high_bit) + 1 - low,
    ]
    kv_at = group - 2 * hd
    partner = (other, b, k)
    sends = []

    def pb_dev(d):
        return (p, lax.rem(b + d, n_pb), k)

    def ka_dev(d):
        return (p, b, lax.rem(k + d, n_ka))

    def b_from(d):
        return lax.rem(b - d + n_pb, n_pb)

    def k_from(d):
        return lax.rem(k - d + n_ka, n_ka)

    def remote(src, dst, name, i, dev):
        at = offsets[name] + i
        return pltpu.make_async_remote_copy(
            src_ref=src, dst_ref=dst, send_sem=ss.at[at], recv_sem=rs.at[at],
            device_id=dev, device_id_type=pl.DeviceIdType.MESH,
        )

    def send(src, dst, name, i, dev):
        copy = remote(src, dst, name, i, dev)
        copy.start()
        sends.append(copy)

    def arrived(dst, name, i):
        remote(dst, dst, name, i, partner).wait_recv()

    def ka_rows(index):
        return pl.ds(pl.multiple_of(index * rows, rows), rows)

    barrier = pltpu.get_barrier_semaphore()
    devs = [partner] + [pb_dev(d) for d in range(1, n_pb)] + [ka_dev(d) for d in range(1, n_ka)]
    for dev in devs:
        pl.semaphore_signal(barrier, inc=1, device_id=dev, device_id_type=pl.DeviceIdType.MESH)
    load = pltpu.make_async_copy(weight_hbm.at[0], wbuf, load_sem)
    load.start()
    pl.semaphore_wait(barrier, len(devs))

    def tok_part(pool, source, h):
        return tokbuf.at[pool, pl.ds(pl.multiple_of(source * rows + h * part, part), part)]

    for e, h in ((1, 0), (2, 1), (1, 1), (2, 0)):
        send(
            tok.at[pl.ds(h * part, part)], tok_part(p, k, h), "tok_ka", 2 * e + h, (p, b, near[e])
        )
    for h in range(2):
        send(tok.at[pl.ds(h * part, part)], tok_part(p, k, h), "tok_fw", h, partner)
    for d in range(1, n_pb):
        send(mod, modbuf.at[b], "mod", d, pb_dev(d))
    tokbuf[p, ka_rows(k), :] = tok[...]
    modbuf[b] = mod[...]

    for i in range(half // 128):
        cols = slice(i * 128, (i + 1) * 128)
        xt[cols, :] = jnp.transpose(tok[:, cols].astype(F32)).astype(BF16)

    def xt_part(target):
        return pl.ds(pl.multiple_of(lax.rem(target, hp) * slice_rows, 16), slice_rows)

    mine = lax.div(b, hp) == p
    for d in range(1, n_pb):
        target = lax.rem(b + d, n_pb)

        @pl.when(lax.div(target, hp) == p)
        def _(d=d, target=target):
            remote(
                xt.at[xt_part(target)], xtbuf.at[b, :, ka_rows(k)], "xt_z", d, pb_dev(d)
            ).start()

    @pl.when(mine)
    def _():
        xtbuf[b, :, ka_rows(k)] = xt[xt_part(b), :]

    def own_mask(index):
        return modbuf[index].astype(F32)[:, :1] == p.astype(F32)

    def hand_on(e, h, relay_to):
        region = tok_part(p, near[e], h)
        arrived(region, "tok_ka", 2 * e + h)
        if relay_to is not None:
            send(region, region, "tok_ka", 6 + h, (p, b, near[relay_to]))
        send(region, region, "tok_fw", 2 * e + h, partner)

    def project(e):
        for h in range(2):
            arrived(tok_part(other, near[e], h), "tok_fw", 2 * e + h)
        at = ka_rows(near[e])
        proj = jnp.dot(tokbuf[0, at, :], wbuf[:half], preferred_element_type=F32)
        proj += jnp.dot(tokbuf[1, at, :], wbuf[half:], preferred_element_type=F32)
        projloc[at, :] = proj.astype(BF16)
        send(projloc.at[at], projrecv.at[at], "pj", e, partner)

    def settle(e):
        at = ka_rows(near[e])
        arrived(projrecv.at[at], "pj", e)
        owned = modbuf[b, at, :].astype(F32)[:, :1] == p.astype(F32)
        projected = jnp.where(owned, projloc[at, :].astype(F32), projrecv[at, :].astype(F32))
        qbuf[at, :] = jnp.where(p == 0, projected[:, :hd], projected[:, hd : 2 * hd]).astype(BF16)
        kvbuf[b, near[e]] = projected[:, kv_at:].astype(BF16).reshape(2, part, 2 * hd)
        region = kvbuf.at[b, near[e], p]
        for d in range(1, n_pb):
            send(region, region, "kv_z", d * n_ka + e, pb_dev(d))

    def pass_keys(e):
        for d in range(1, n_pb):
            region = kvbuf.at[b_from(d), near[e], p]
            arrived(region, "kv_z", d * n_ka + e)
            send(region, region, "kv_fw", d * n_ka + e, partner)

    load.wait()
    project(0)
    hand_on(1, 0, 2)
    hand_on(2, 1, 1)
    settle(0)
    hand_on(1, 1, None)
    hand_on(2, 0, None)
    project(1)
    project(2)
    settle(1)
    settle(2)
    pass_keys(0)
    hand_on(3, 0, None)
    hand_on(3, 1, None)
    project(3)

    @pl.when(mine)
    def _():
        for d in range(1, n_pb):
            arrived(xtbuf.at[b_from(d), :, ka_rows(k)], "xt_z", d)
        for d in range(1, n_ka):
            region = xtbuf.at[:, :, ka_rows(k)]
            remote(region, region, "xt_ka", d, ka_dev(d)).start()
        region = xtbuf.at[:, :, ka_rows(k)]
        remote(region, region, "xt_fw", 0, partner).start()

    settle(3)
    for e in range(1, n_ka):
        pass_keys(e)
    for e in range(n_ka):
        for d in range(1, n_pb):
            arrived(kvbuf.at[b_from(d), near[e], other], "kv_fw", d * n_ka + e)

    keys = n_pb * q_rows
    key_rows = kvbuf[:, :, :, :, :hd].reshape(keys, hd)
    ktbuf[...] = jnp.transpose(key_rows.astype(F32)).astype(BF16)
    tile = min(256, q_rows)
    for t in range(q_rows // tile):
        at = slice(t * tile, (t + 1) * tile)
        key_rows = kvbuf[:, :, :, :, :hd].reshape(keys, hd)
        value_rows = kvbuf[:, :, :, :, hd:].reshape(keys, hd)
        scores = lax.dot_general(key_rows, qbuf[at, :], NT, preferred_element_type=F32) * scaling
        high = jnp.max(scores, axis=0, keepdims=True)
        raised = jnp.exp(scores - high)
        softmax = raised * (1.0 / jnp.sum(raised, axis=0, keepdims=True))
        grad_prob = lax.dot_general(value_rows, cot[0, at, :], NT, preferred_element_type=F32)
        delta = jnp.sum(softmax * grad_prob, axis=0, keepdims=True)
        grad_score = (softmax * (grad_prob - delta)).astype(BF16)
        prob[:, :, at] = softmax.astype(BF16).reshape(n_pb, q_rows, tile)
        score[:, :, at] = grad_score.reshape(n_pb, q_rows, tile)

    def key_block(d):
        block = lax.rem(b + d, n_pb)
        dk = jnp.dot(score[block], qbuf[...], preferred_element_type=F32) * scaling
        dv = jnp.dot(prob[block], cot[0], preferred_element_type=F32)
        dkv[block, :, :, :hd] = dk.astype(BF16).reshape(2, q_half, hd)
        dkv[block, :, :, hd:] = dv.astype(BF16).reshape(2, q_half, hd)
        send(dkv.at[block, other], dkvp.at[block], "dk_p", d, partner)

    def key_sum(d):
        block = lax.rem(b + d, n_pb)
        arrived(dkvp.at[block], "dk_p", d)
        dkvs[block] = (dkv[block, p].astype(F32) + dkvp[block].astype(F32)).astype(BF16)
        if d:
            send(dkvs.at[block], dkvr.at[d], "dk_z", d, pb_dev(d))

    turns = list(range(1, n_pb)) + [0]
    for i, d in enumerate(turns):
        key_block(d)
        if i:
            key_sum(turns[i - 1])
    key_sum(0)
    dq = jnp.dot(ktbuf[...], score[...].reshape(keys, q_rows), preferred_element_type=F32) * scaling
    dq = jnp.transpose(dq).astype(BF16)

    @pl.when(p == 0)
    def _():
        gp[b, :, :hd] = dq

    @pl.when(p == 1)
    def _():
        gp[b, :, hd : 2 * hd] = dq

    def q_cols(pool):
        return pl.ds(pl.multiple_of(pool * hd, hd), hd)

    def half_rows(pool):
        return pl.ds(pl.multiple_of(pool * q_half, q_half), q_half)

    dq_own = gp.at[b, :, q_cols(p)]
    send(dq_own, dq_own, "dq_p", 0, partner)
    for d in range(1, n_pb):
        send(dq_own, dq_own, "dq_z", d, pb_dev(d))

    @pl.when(mine)
    def _():
        for d in range(1, n_ka):
            region = xtbuf.at[:, :, ka_rows(k_from(d))]
            arrived(region, "xt_ka", d)
            remote(region, region, "xt_fw", d, partner).start()

    total = dkvs[b].astype(F32)
    for d in range(1, n_pb):
        arrived(dkvr.at[d], "dk_z", d)
        total += dkvr[d].astype(F32)
    gp[b, half_rows(p), kv_at:] = total.astype(BF16)
    kv_own = gp.at[b, half_rows(p), pl.ds(kv_at, 2 * hd)]
    send(kv_own, kv_own, "gk_p", 0, partner)
    for d in range(1, n_pb):
        send(kv_own, kv_own, "gk_z", d, pb_dev(d))
    arrived(gp.at[b, :, q_cols(other)], "dq_p", 0)
    arrived(gp.at[b, half_rows(other), pl.ds(kv_at, 2 * hd)], "gk_p", 0)

    mgp[b] = jnp.where(own_mask(b), gp[b].astype(F32), 0.0).astype(BF16)

    def relayed(e, c):
        h = 2 - e
        arrived(rel.at[h, c], "rel", h * n_c + c)
        at = pl.ds(pl.multiple_of(near[e] * rows + h * part, part), part)
        bsum[c, at, :] = (bsum[c, at, :].astype(F32) + rel[h, c].astype(F32)).astype(BF16)
        return partial_copy(e, h, c)

    def partial_copy(e, h, c):
        at = pl.ds(pl.multiple_of(near[e] * rows + h * part, part), part)
        return remote(
            bsum.at[c, at], kar.at[e - 1, c, pl.ds(h * part, part)],
            "kar", (2 * (e - 1) + h) * n_c + c, (p, b, near[e]),
        )

    def relay_copy(h, c):
        at = pl.ds(pl.multiple_of(near[3] * rows + h * part, part), part)
        return remote(bsum.at[c, at], rel.at[h, c], "rel", h * n_c + c, (p, b, near[1 + h]))

    def back_chunk(c, carry):
        def product(pool):
            at = pl.ds(pl.multiple_of(pool * half + c * chunk, 128), chunk)
            return lax.dot_general(mgp[b], wbuf[at, :], NT, preferred_element_type=F32)

        bsend[c] = product(other).astype(BF16)
        remote(bsend.at[c], brecv.at[c], "bk_p", c, partner).start()
        own = product(p).astype(BF16).astype(F32)
        arrived(brecv.at[c], "bk_p", c)
        bsum[c] = (own + brecv[c].astype(F32)).astype(BF16)
        for h in range(2):
            relay_copy(h, c).start()
        partial_copy(1, 0, c).start()
        partial_copy(2, 1, c).start()

        @pl.when(c > 0)
        def _():
            for e in (2, 1):
                relayed(e, c - 1).start()

        return carry

    lax.fori_loop(0, n_c, back_chunk, 0)
    for e in (2, 1):
        relayed(e, n_c - 1).start()

    for d in range(1, n_pb):
        region = gp.at[b_from(d), :, q_cols(p)]
        arrived(region, "dq_z", d)
        send(region, region, "dq_p", d, partner)
    for d in range(1, n_pb):
        region = gp.at[b_from(d), half_rows(p), pl.ds(kv_at, 2 * hd)]
        arrived(region, "gk_z", d)
        send(region, region, "gk_p", d, partner)
    for d in range(1, n_pb):
        arrived(modbuf.at[b_from(d)], "mod", d)
    for d in range(1, n_pb):
        arrived(gp.at[b_from(d), :, q_cols(other)], "dq_p", d)
        arrived(gp.at[b_from(d), half_rows(other), pl.ds(kv_at, 2 * hd)], "gk_p", d)
        source = b_from(d)
        mgp[source] = jnp.where(own_mask(source), gp[source].astype(F32), 0.0).astype(BF16)

    @pl.when(jnp.logical_not(mine))
    def _():
        for d in range(n_ka):
            arrived(xtbuf.at[:, :, ka_rows(k_from(d))], "xt_fw", d)

    w_tile = divisor(slice_rows, 16, 512)

    def weight_rows(t, carry):
        at = pl.ds(pl.multiple_of(t * w_tile, 16), w_tile)
        acc = jnp.dot(xtbuf[0, at, :], mgp[0], preferred_element_type=F32)
        for i in range(1, n_pb):
            acc += jnp.dot(xtbuf[i, at, :], mgp[i], preferred_element_type=F32)
        wout[at, :] = acc
        return carry

    lax.fori_loop(0, slice_rows // w_tile, weight_rows, 0)
    store = pltpu.make_async_copy(wout, out_weight.at[0], store_sem)
    store.start()

    for c in range(n_c):
        acc = bsum[c, ka_rows(k), :].astype(F32)
        for e in (1, 2):
            for h in range(2):
                arrived(kar.at[e - 1, c, pl.ds(h * part, part)], "kar", (2 * (e - 1) + h) * n_c + c)
            acc += kar[e - 1, c].astype(F32)
        out_tok[:, c * chunk : (c + 1) * chunk] = acc.astype(BF16)

    store.wait()
    for copy in sends:
        copy.wait_send()
    for d in range(1, n_pb):
        target = lax.rem(b + d, n_pb)

        @pl.when(lax.div(target, hp) == p)
        def _(d=d, target=target):
            remote(xt.at[xt_part(target)], xtbuf.at[b, :, ka_rows(k)], "xt_z", d, pb_dev(d)).wait_send()

    @pl.when(mine)
    def _():
        region = xtbuf.at[:, :, ka_rows(k)]
        for d in range(1, n_ka):
            remote(region, region, "xt_ka", d, ka_dev(d)).wait_send()
        for d in range(n_ka):
            region = xtbuf.at[:, :, ka_rows(k_from(d))]
            remote(region, region, "xt_fw", d, partner).wait_send()

    def sent(c, carry):
        remote(bsend.at[c], brecv.at[c], "bk_p", c, partner).wait_send()
        for h in range(2):
            relay_copy(h, c).wait_send()
            for e in (1, 2):
                partial_copy(e, h, c).wait_send()
        return carry

    lax.fori_loop(0, n_c, sent, 0)


def shards(tokens, modality, proj_weight, out_grad):
    n_pool, n_pb, n_ka = (lax.axis_size(name) for name in ("pool", "pb", "ka"))
    rows, half = tokens.shape
    group = proj_weight.shape[2]
    width = proj_weight.shape[1]
    q_rows, hd = out_grad.shape[1:]
    keys = n_pb * q_rows
    slice_rows = width // n_pb
    chunk = divisor(half, 128, 512)
    n_c = half // chunk
    vmem, scratch_bytes = [], 0
    shapes = [
        ((2, q_rows, half), BF16), ((width, group), BF16), ((n_pb, slice_rows, q_rows), BF16),
        ((n_pb, q_rows, hd), BF16), ((q_rows, group), BF16), ((q_rows, group), BF16),
        ((q_rows, hd), BF16), ((n_pb, n_ka, 2, rows // 2, 2 * hd), BF16), ((hd, keys), BF16),
        ((n_pb, q_rows, q_rows), BF16), ((n_pb, q_rows, q_rows), BF16), ((n_pb, 2, q_rows // 2, 2 * hd), BF16),
        ((n_pb, q_rows // 2, 2 * hd), BF16), ((n_pb, q_rows // 2, 2 * hd), BF16),
        ((n_pb, q_rows // 2, 2 * hd), BF16), ((n_pb, q_rows, group), BF16),
        ((n_pb, q_rows, group), BF16), ((n_c, q_rows, chunk), BF16), ((n_c, q_rows, chunk), BF16),
        ((n_c, q_rows, chunk), BF16), ((2, n_c, rows, chunk), BF16),
        ((2, n_c, rows // 2, chunk), BF16), ((half, rows), BF16), ((slice_rows, group), F32),
    ]
    for shape, kind in shapes:
        vmem.append(pltpu.VMEM(shape, kind))
        scratch_bytes += math.prod(shape) * jnp.dtype(kind).itemsize
    scratch_bytes += 5 * keys * min(256, q_rows) * 4
    if scratch_bytes > 58 * 2**20 or n_pool != 2 or n_pb % 2 or n_ka != 4:
        return plain_shards(tokens, modality, proj_weight, out_grad)
    offsets, count = {}, 0
    for name, size in (
        ("tok_ka", 2 * n_ka), ("tok_fw", 2 * n_ka), ("mod", n_pb), ("xt_z", n_pb), ("xt_ka", n_ka),
        ("xt_fw", n_ka), ("pj", n_ka), ("kv_z", n_pb * n_ka), ("kv_fw", n_pb * n_ka), ("dk_p", n_pb), ("dk_z", n_pb),
        ("dq_p", n_pb), ("dq_z", n_pb), ("gk_p", n_pb), ("gk_z", n_pb), ("bk_p", n_c),
        ("kar", 4 * n_c), ("rel", 2 * n_c),
    ):
        offsets[name] = count
        count += size
    dims = (n_pb, n_ka, rows, half, group, hd, q_rows, offsets)
    in_vmem = pl.BlockSpec(memory_space=pltpu.VMEM)
    kinds = jnp.broadcast_to(modality.astype(BF16)[:, None], (q_rows, hd))
    return pl.pallas_call(
        functools.partial(fused, dims),
        out_shape=(
            jax.ShapeDtypeStruct((rows, half), BF16),
            jax.ShapeDtypeStruct((1, slice_rows, group), F32),
        ),
        in_specs=[in_vmem, in_vmem, pl.BlockSpec(memory_space=pl.ANY), in_vmem],
        out_specs=(in_vmem, pl.BlockSpec(memory_space=pl.ANY)),
        scratch_shapes=vmem
        + [
            pltpu.SemaphoreType.DMA,
            pltpu.SemaphoreType.DMA,
            pltpu.SemaphoreType.DMA((count,)),
            pltpu.SemaphoreType.DMA((count,)),
        ],
        compiler_params=pltpu.CompilerParams(
            collective_id=0, has_side_effects=True, vmem_limit_bytes=62 * 2**20
        ),
    )(tokens, kinds, proj_weight, out_grad)


def solution(mesh):
    return jax.shard_map(
        shards,
        mesh=mesh,
        in_specs=(P(("pb", "ka"), "pool"), P("pb"), P("pool", None, "ka"), P("pool", "pb", "ka")),
        out_specs=(P(("pb", "ka"), "pool"), P("pool", "pb", "ka")),
        check_vma=False,
    )
```

```python
import functools
import math

import jax
import jax.numpy as jnp
from jax import lax
from jax.experimental import pallas as pl
from jax.experimental.pallas import tpu as pltpu
from jax.sharding import PartitionSpec as P


def plain_shards(tokens, modality, proj_weight, out_grad):
    contract_one = (((1,), (1,)), ((), ()))
    contract_zero = (((0,), (0,)), ((), ()))
    pool_index = lax.axis_index("pool")
    pool_count = lax.axis_size("pool")
    head_size = out_grad.shape[2]
    scaling = 1.0 / math.sqrt(head_size)
    token_count = tokens.shape[0]
    half_width = tokens.shape[1]
    group_width = proj_weight.shape[2]
    weight = proj_weight[0].reshape(pool_count, half_width, group_width)
    gathered = lax.all_gather(tokens[None], ("pool", "ka"), axis=0, tiled=True)
    query_count = gathered.shape[0] // pool_count * token_count
    block_tokens = gathered.reshape(pool_count, query_count, half_width)
    owned = (modality == pool_index)[:, None]
    local_proj = jnp.where(
        owned,
        lax.dot_general(
            block_tokens, weight, (((0, 2), (0, 1)), ((), ())), preferred_element_type=jnp.float32
        ),
        0.0,
    )
    projected = lax.psum(local_proj.astype(jnp.bfloat16), "pool")
    queries = lax.dynamic_slice_in_dim(projected, pool_index * head_size, head_size, 1)
    half_rows = query_count // pool_count
    own_keys = projected[:, group_width - 2 * head_size :].reshape(
        pool_count, half_rows, 2 * head_size
    )
    key_value = lax.all_gather(own_keys, "pb", axis=1, tiled=True).reshape(-1, 2 * head_size)
    key_rows = key_value[:, :head_size]
    value_rows = key_value[:, head_size:]
    cotangent = out_grad[0]
    tile_rows = min(512, query_count)
    tile_count = query_count // tile_rows
    q_tiles = queries.reshape(tile_count, tile_rows, head_size)
    o_tiles = cotangent.reshape(tile_count, tile_rows, head_size)

    def advance(running, tile_in):
        q_tile, o_tile = tile_in
        scores = (
            lax.dot_general(q_tile, key_rows, contract_one, preferred_element_type=jnp.float32)
            * scaling
        )
        row_max = jnp.max(scores, axis=1, keepdims=True)
        log_total = row_max + jnp.log(jnp.sum(jnp.exp(scores - row_max), axis=1, keepdims=True))
        softmax = jnp.exp(scores - log_total)
        grad_prob = lax.dot_general(
            o_tile, value_rows, contract_one, preferred_element_type=jnp.float32
        )
        delta = jnp.sum(softmax * grad_prob, axis=1, keepdims=True)
        grad_score = (softmax * (grad_prob - delta)).astype(jnp.bfloat16)
        grad_query = jnp.dot(grad_score, key_rows, preferred_element_type=jnp.float32) * scaling
        new_keys = (
            running[0]
            + lax.dot_general(grad_score, q_tile, contract_zero, preferred_element_type=jnp.float32)
            * scaling
        )
        new_values = running[1] + lax.dot_general(
            softmax.astype(jnp.bfloat16), o_tile, contract_zero, preferred_element_type=jnp.float32
        )
        return ((new_keys, new_values), grad_query)

    key_count = key_rows.shape[0]
    start_state = (
        jnp.zeros((key_count, head_size), jnp.float32),
        jnp.zeros((key_count, head_size), jnp.float32),
    )
    (grad_keys, grad_values), grad_query = lax.scan(advance, start_state, (q_tiles, o_tiles))
    key_terms = jnp.concatenate([grad_keys, grad_values], axis=1)
    key_cell = lax.psum_scatter(
        key_terms.astype(jnp.bfloat16), ("pool", "pb"), scatter_dimension=0, tiled=True
    )
    query_low = grad_query.reshape(query_count, head_size).astype(jnp.bfloat16)
    both_queries, key_block = (
        lax.all_gather(query_low, "pool", axis=1, tiled=True),
        lax.all_gather(key_cell, "pool", axis=0, tiled=True),
    )
    grad_proj = jnp.concatenate([both_queries, key_block], axis=1)
    masked = jnp.where(owned, grad_proj, jnp.zeros_like(grad_proj))
    back = jnp.einsum("rj,pcj->prc", masked, weight, preferred_element_type=jnp.float32)
    stacked = back.reshape(pool_count * (query_count // token_count), token_count, half_width)
    token_sum = lax.psum_scatter(
        stacked.astype(jnp.bfloat16), ("pool", "ka"), scatter_dimension=0, tiled=True
    ).astype(jnp.float32)[0]
    grad_tokens = token_sum.astype(jnp.bfloat16)
    term = jnp.einsum(
        "prc,rj->pcj", block_tokens, masked, preferred_element_type=jnp.float32
    ).reshape(-1, group_width)
    grad_weight = lax.psum_scatter(
        term.astype(jnp.bfloat16), "pb", scatter_dimension=0, tiled=True
    ).astype(jnp.float32)
    return (grad_tokens, grad_weight[None])


BF16 = jnp.bfloat16
F32 = jnp.float32
NT = (((1,), (1,)), ((), ()))


def divisor(total, unit, most):
    best = unit
    for size in range(unit, most + 1, unit):
        if total % size == 0:
            best = size
    return best


def fused(
    dims, tok, mod, weight_hbm, cot, out_tok, out_weight,
    tokbuf, wbuf, xtbuf, modbuf, projloc, projrecv, qbuf, kvbuf, ktbuf, prob, score,
    dkv, dkvp, dkvs, dkvr, gp, mgp, bsend, brecv, bsum, kar, rel, xt, wout, load_sem, store_sem, ss, rs,
):
    n_pb, n_ka, rows, half, group, hd, q_rows, offsets = dims
    scaling = 1.0 / math.sqrt(hd)
    p, b, k = lax.axis_index("pool"), lax.axis_index("pb"), lax.axis_index("ka")
    other = 1 - p
    q_half = q_rows // 2
    hp = n_pb // 2
    n_c, chunk = bsend.shape[0], bsend.shape[2]
    slice_rows = xtbuf.shape[1]
    part = rows // 2
    low, high_bit = lax.rem(k, 2), lax.div(k, 2)
    near = [
        k,
        2 * high_bit + 1 - low,
        2 * (1 - high_bit) + low,
        2 * (1 - high_bit) + 1 - low,
    ]
    kv_at = group - 2 * hd
    partner = (other, b, k)
    sends = []

    def pb_dev(d):
        return (p, lax.rem(b + d, n_pb), k)

    def ka_dev(d):
        return (p, b, lax.rem(k + d, n_ka))

    def b_from(d):
        return lax.rem(b - d + n_pb, n_pb)

    def k_from(d):
        return lax.rem(k - d + n_ka, n_ka)

    def remote(src, dst, name, i, dev):
        at = offsets[name] + i
        return pltpu.make_async_remote_copy(
            src_ref=src, dst_ref=dst, send_sem=ss.at[at], recv_sem=rs.at[at],
            device_id=dev, device_id_type=pl.DeviceIdType.MESH,
        )

    def send(src, dst, name, i, dev):
        copy = remote(src, dst, name, i, dev)
        copy.start()
        sends.append(copy)

    def arrived(dst, name, i):
        remote(dst, dst, name, i, partner).wait_recv()

    def ka_rows(index):
        return pl.ds(pl.multiple_of(index * rows, rows), rows)

    barrier = pltpu.get_barrier_semaphore()
    devs = [partner] + [pb_dev(d) for d in range(1, n_pb)] + [ka_dev(d) for d in range(1, n_ka)]
    for dev in devs:
        pl.semaphore_signal(barrier, inc=1, device_id=dev, device_id_type=pl.DeviceIdType.MESH)
    load = pltpu.make_async_copy(weight_hbm.at[0], wbuf, load_sem)
    load.start()
    pl.semaphore_wait(barrier, len(devs))

    def tok_part(pool, source, h):
        return tokbuf.at[pool, pl.ds(pl.multiple_of(source * rows + h * part, part), part)]

    for e, h in ((1, 0), (2, 1), (1, 1), (2, 0)):
        send(
            tok.at[pl.ds(h * part, part)], tok_part(p, k, h), "tok_ka", 2 * e + h, (p, b, near[e])
        )
    for h in range(2):
        send(tok.at[pl.ds(h * part, part)], tok_part(p, k, h), "tok_fw", h, partner)
    for d in range(1, n_pb):
        send(mod, modbuf.at[b], "mod", d, pb_dev(d))
    tokbuf[p, ka_rows(k), :] = tok[...]
    modbuf[b] = mod[...]

    for i in range(half // 128):
        cols = slice(i * 128, (i + 1) * 128)
        xt[cols, :] = jnp.transpose(tok[:, cols].astype(F32)).astype(BF16)

    def xt_part(target):
        return pl.ds(pl.multiple_of(lax.rem(target, hp) * slice_rows, 16), slice_rows)

    mine = lax.div(b, hp) == p
    for d in range(1, n_pb):
        target = lax.rem(b + d, n_pb)

        @pl.when(lax.div(target, hp) == p)
        def _(d=d, target=target):
            remote(
                xt.at[xt_part(target)], xtbuf.at[b, :, ka_rows(k)], "xt_z", d, pb_dev(d)
            ).start()

    @pl.when(mine)
    def _():
        xtbuf[b, :, ka_rows(k)] = xt[xt_part(b), :]

    def own_mask(index):
        return modbuf[index].astype(F32)[:, :1] == p.astype(F32)

    def hand_on(e, h, relay_to):
        region = tok_part(p, near[e], h)
        arrived(region, "tok_ka", 2 * e + h)
        if relay_to is not None:
            send(region, region, "tok_ka", 6 + h, (p, b, near[relay_to]))
        send(region, region, "tok_fw", 2 * e + h, partner)

    def project(e):
        for h in range(2):
            arrived(tok_part(other, near[e], h), "tok_fw", 2 * e + h)
        at = ka_rows(near[e])
        proj = jnp.dot(tokbuf[0, at, :], wbuf[:half], preferred_element_type=F32)
        proj += jnp.dot(tokbuf[1, at, :], wbuf[half:], preferred_element_type=F32)
        projloc[at, :] = proj.astype(BF16)
        send(projloc.at[at], projrecv.at[at], "pj", e, partner)

    def settle(e):
        at = ka_rows(near[e])
        arrived(projrecv.at[at], "pj", e)
        owned = modbuf[b, at, :].astype(F32)[:, :1] == p.astype(F32)
        projected = jnp.where(owned, projloc[at, :].astype(F32), projrecv[at, :].astype(F32))
        qbuf[at, :] = jnp.where(p == 0, projected[:, :hd], projected[:, hd : 2 * hd]).astype(BF16)
        kvbuf[b, near[e]] = projected[:, kv_at:].astype(BF16).reshape(2, part, 2 * hd)
        region = kvbuf.at[b, near[e], p]
        for d in range(1, n_pb):
            send(region, region, "kv_z", d * n_ka + e, pb_dev(d))

    def pass_keys(e):
        for d in range(1, n_pb):
            region = kvbuf.at[b_from(d), near[e], p]
            arrived(region, "kv_z", d * n_ka + e)
            send(region, region, "kv_fw", d * n_ka + e, partner)

    load.wait()
    project(0)
    hand_on(1, 0, 2)
    hand_on(2, 1, 1)
    settle(0)
    hand_on(1, 1, None)
    hand_on(2, 0, None)
    project(1)
    project(2)
    settle(1)
    settle(2)
    pass_keys(0)
    hand_on(3, 0, None)
    hand_on(3, 1, None)
    project(3)

    @pl.when(mine)
    def _():
        for d in range(1, n_pb):
            arrived(xtbuf.at[b_from(d), :, ka_rows(k)], "xt_z", d)
        for d in range(1, n_ka):
            region = xtbuf.at[:, :, ka_rows(k)]
            remote(region, region, "xt_ka", d, ka_dev(d)).start()
        region = xtbuf.at[:, :, ka_rows(k)]
        remote(region, region, "xt_fw", 0, partner).start()

    settle(3)
    for e in range(1, n_ka):
        pass_keys(e)
    for e in range(n_ka):
        for d in range(1, n_pb):
            arrived(kvbuf.at[b_from(d), near[e], other], "kv_fw", d * n_ka + e)

    keys = n_pb * q_rows
    key_rows = kvbuf[:, :, :, :, :hd].reshape(keys, hd)
    ktbuf[...] = jnp.transpose(key_rows.astype(F32)).astype(BF16)
    tile = min(256, q_rows)
    for t in range(q_rows // tile):
        at = slice(t * tile, (t + 1) * tile)
        key_rows = kvbuf[:, :, :, :, :hd].reshape(keys, hd)
        value_rows = kvbuf[:, :, :, :, hd:].reshape(keys, hd)
        scores = lax.dot_general(key_rows, qbuf[at, :], NT, preferred_element_type=F32)
        high = jnp.max(scores, axis=0, keepdims=True)
        raised = jnp.exp((scores - high) * scaling)
        softmax = raised * (1.0 / jnp.sum(raised, axis=0, keepdims=True))
        grad_prob = lax.dot_general(value_rows, cot[0, at, :], NT, preferred_element_type=F32)
        delta = jnp.sum(softmax * grad_prob, axis=0, keepdims=True)
        grad_score = (softmax * (grad_prob - delta)).astype(BF16)
        prob[:, :, at] = softmax.astype(BF16).reshape(n_pb, q_rows, tile)
        score[:, :, at] = grad_score.reshape(n_pb, q_rows, tile)

    def key_block(d):
        block = lax.rem(b + d, n_pb)
        dk = jnp.dot(score[block], qbuf[...], preferred_element_type=F32) * scaling
        dv = jnp.dot(prob[block], cot[0], preferred_element_type=F32)
        dkv[block, :, :, :hd] = dk.astype(BF16).reshape(2, q_half, hd)
        dkv[block, :, :, hd:] = dv.astype(BF16).reshape(2, q_half, hd)
        send(dkv.at[block, other], dkvp.at[block], "dk_p", d, partner)

    def key_sum(d):
        block = lax.rem(b + d, n_pb)
        arrived(dkvp.at[block], "dk_p", d)
        dkvs[block] = (dkv[block, p].astype(F32) + dkvp[block].astype(F32)).astype(BF16)
        if d:
            send(dkvs.at[block], dkvr.at[d], "dk_z", d, pb_dev(d))

    turns = list(range(1, n_pb)) + [0]
    for i, d in enumerate(turns):
        key_block(d)
        if i:
            key_sum(turns[i - 1])
    key_sum(0)
    dq = jnp.dot(ktbuf[...], score[...].reshape(keys, q_rows), preferred_element_type=F32) * scaling
    dq = jnp.transpose(dq).astype(BF16)

    @pl.when(p == 0)
    def _():
        gp[b, :, :hd] = dq

    @pl.when(p == 1)
    def _():
        gp[b, :, hd : 2 * hd] = dq

    def q_cols(pool):
        return pl.ds(pl.multiple_of(pool * hd, hd), hd)

    def half_rows(pool):
        return pl.ds(pl.multiple_of(pool * q_half, q_half), q_half)

    dq_own = gp.at[b, :, q_cols(p)]
    send(dq_own, dq_own, "dq_p", 0, partner)
    for d in range(1, n_pb):
        send(dq_own, dq_own, "dq_z", d, pb_dev(d))

    @pl.when(mine)
    def _():
        for d in range(1, n_ka):
            region = xtbuf.at[:, :, ka_rows(k_from(d))]
            arrived(region, "xt_ka", d)
            remote(region, region, "xt_fw", d, partner).start()

    total = dkvs[b].astype(F32)
    for d in range(1, n_pb):
        arrived(dkvr.at[d], "dk_z", d)
        total += dkvr[d].astype(F32)
    gp[b, half_rows(p), kv_at:] = total.astype(BF16)
    kv_own = gp.at[b, half_rows(p), pl.ds(kv_at, 2 * hd)]
    send(kv_own, kv_own, "gk_p", 0, partner)
    for d in range(1, n_pb):
        send(kv_own, kv_own, "gk_z", d, pb_dev(d))
    arrived(gp.at[b, :, q_cols(other)], "dq_p", 0)
    arrived(gp.at[b, half_rows(other), pl.ds(kv_at, 2 * hd)], "gk_p", 0)

    mgp[b] = jnp.where(own_mask(b), gp[b].astype(F32), 0.0).astype(BF16)

    def relayed(e, c):
        h = 2 - e
        arrived(rel.at[h, c], "rel", h * n_c + c)
        at = pl.ds(pl.multiple_of(near[e] * rows + h * part, part), part)
        bsum[c, at, :] = (bsum[c, at, :].astype(F32) + rel[h, c].astype(F32)).astype(BF16)
        return partial_copy(e, h, c)

    def partial_copy(e, h, c):
        at = pl.ds(pl.multiple_of(near[e] * rows + h * part, part), part)
        return remote(
            bsum.at[c, at], kar.at[e - 1, c, pl.ds(h * part, part)],
            "kar", (2 * (e - 1) + h) * n_c + c, (p, b, near[e]),
        )

    def relay_copy(h, c):
        at = pl.ds(pl.multiple_of(near[3] * rows + h * part, part), part)
        return remote(bsum.at[c, at], rel.at[h, c], "rel", h * n_c + c, (p, b, near[1 + h]))

    def back_chunk(c, carry):
        def product(pool):
            at = pl.ds(pl.multiple_of(pool * half + c * chunk, 128), chunk)
            return lax.dot_general(mgp[b], wbuf[at, :], NT, preferred_element_type=F32)

        bsend[c] = product(other).astype(BF16)
        remote(bsend.at[c], brecv.at[c], "bk_p", c, partner).start()
        bsum[c] = product(p).astype(BF16)

        @pl.when(c > 0)
        def _():
            pool_sum(c - 1)

        return carry

    def pool_sum(c):
        arrived(brecv.at[c], "bk_p", c)
        bsum[c] = (bsum[c].astype(F32) + brecv[c].astype(F32)).astype(BF16)
        for h in range(2):
            relay_copy(h, c).start()
        partial_copy(1, 0, c).start()
        partial_copy(2, 1, c).start()

    def relay_sums(c):
        for e in (2, 1):
            relayed(e, c).start()

    lax.fori_loop(0, n_c, back_chunk, 0)
    pool_sum(n_c - 1)
    relay_sums(0)

    for d in range(1, n_pb):
        region = gp.at[b_from(d), :, q_cols(p)]
        arrived(region, "dq_z", d)
        send(region, region, "dq_p", d, partner)
    for d in range(1, n_pb):
        region = gp.at[b_from(d), half_rows(p), pl.ds(kv_at, 2 * hd)]
        arrived(region, "gk_z", d)
        send(region, region, "gk_p", d, partner)
    for d in range(1, n_pb):
        arrived(modbuf.at[b_from(d)], "mod", d)
    for d in range(1, n_pb):
        arrived(gp.at[b_from(d), :, q_cols(other)], "dq_p", d)
        arrived(gp.at[b_from(d), half_rows(other), pl.ds(kv_at, 2 * hd)], "gk_p", d)
        source = b_from(d)
        mgp[source] = jnp.where(own_mask(source), gp[source].astype(F32), 0.0).astype(BF16)

    @pl.when(jnp.logical_not(mine))
    def _():
        for d in range(n_ka):
            arrived(xtbuf.at[:, :, ka_rows(k_from(d))], "xt_fw", d)

    tiles = n_c - 1 if n_c > 1 and slice_rows % (16 * (n_c - 1)) == 0 else 1
    w_tile = slice_rows // tiles

    def weight_rows(t):
        at = pl.ds(pl.multiple_of(t * w_tile, 16), w_tile)
        acc = jnp.dot(xtbuf[0, at, :], mgp[0], preferred_element_type=F32)
        for i in range(1, n_pb):
            acc += jnp.dot(xtbuf[i, at, :], mgp[i], preferred_element_type=F32)
        wout[at, :] = acc

    def weight_and_relay(t, carry):
        relay_sums(t + 1)

        @pl.when(t < tiles)
        def _():
            weight_rows(t)

        return carry

    lax.fori_loop(0, n_c - 1, weight_and_relay, 0)
    if n_c == 1:
        weight_rows(0)
    store = pltpu.make_async_copy(wout, out_weight.at[0], store_sem)
    store.start()

    for c in range(n_c):
        acc = bsum[c, ka_rows(k), :].astype(F32)
        for e in (1, 2):
            for h in range(2):
                arrived(kar.at[e - 1, c, pl.ds(h * part, part)], "kar", (2 * (e - 1) + h) * n_c + c)
            acc += kar[e - 1, c].astype(F32)
        out_tok[:, c * chunk : (c + 1) * chunk] = acc.astype(BF16)

    store.wait()
    for copy in sends:
        copy.wait_send()
    for d in range(1, n_pb):
        target = lax.rem(b + d, n_pb)

        @pl.when(lax.div(target, hp) == p)
        def _(d=d, target=target):
            remote(xt.at[xt_part(target)], xtbuf.at[b, :, ka_rows(k)], "xt_z", d, pb_dev(d)).wait_send()

    @pl.when(mine)
    def _():
        region = xtbuf.at[:, :, ka_rows(k)]
        for d in range(1, n_ka):
            remote(region, region, "xt_ka", d, ka_dev(d)).wait_send()
        for d in range(n_ka):
            region = xtbuf.at[:, :, ka_rows(k_from(d))]
            remote(region, region, "xt_fw", d, partner).wait_send()

    def sent(c, carry):
        remote(bsend.at[c], brecv.at[c], "bk_p", c, partner).wait_send()
        for h in range(2):
            relay_copy(h, c).wait_send()
            for e in (1, 2):
                partial_copy(e, h, c).wait_send()
        return carry

    lax.fori_loop(0, n_c, sent, 0)


def hand_over(tok_from, weight_from, tok_to, weight_to, sems):
    count = sems.shape[0]
    copies = []
    for source, target, first, parts in (
        (tok_from, tok_to, 0, 2),
        (weight_from.at[0], weight_to.at[0], 2, count - 2),
    ):
        if source.shape[0] % (8 * parts * 2):
            parts = 1
        rows = source.shape[0] // parts
        for i in range(parts):
            at = pl.ds(i * rows, rows)
            copies.append(pltpu.make_async_copy(source.at[at], target.at[at], sems.at[first + i]))
    for copy in copies:
        copy.start()
    for copy in copies:
        copy.wait()


def shards(tokens, modality, proj_weight, out_grad):
    n_pool, n_pb, n_ka = (lax.axis_size(name) for name in ("pool", "pb", "ka"))
    rows, half = tokens.shape
    group = proj_weight.shape[2]
    width = proj_weight.shape[1]
    q_rows, hd = out_grad.shape[1:]
    keys = n_pb * q_rows
    slice_rows = width // n_pb
    chunk = divisor(half, 128, 512)
    n_c = half // chunk
    vmem, scratch_bytes = [], 0
    shapes = [
        ((2, q_rows, half), BF16), ((width, group), BF16), ((n_pb, slice_rows, q_rows), BF16),
        ((n_pb, q_rows, hd), BF16), ((q_rows, group), BF16), ((q_rows, group), BF16),
        ((q_rows, hd), BF16), ((n_pb, n_ka, 2, rows // 2, 2 * hd), BF16), ((hd, keys), BF16),
        ((n_pb, q_rows, q_rows), BF16), ((n_pb, q_rows, q_rows), BF16), ((n_pb, 2, q_rows // 2, 2 * hd), BF16),
        ((n_pb, q_rows // 2, 2 * hd), BF16), ((n_pb, q_rows // 2, 2 * hd), BF16),
        ((n_pb, q_rows // 2, 2 * hd), BF16), ((n_pb, q_rows, group), BF16),
        ((n_pb, q_rows, group), BF16), ((n_c, q_rows, chunk), BF16), ((n_c, q_rows, chunk), BF16),
        ((n_c, q_rows, chunk), BF16), ((2, n_c, rows, chunk), BF16),
        ((2, n_c, rows // 2, chunk), BF16), ((half, rows), BF16), ((slice_rows, group), F32),
    ]
    for shape, kind in shapes:
        vmem.append(pltpu.VMEM(shape, kind))
        scratch_bytes += math.prod(shape) * jnp.dtype(kind).itemsize
    scratch_bytes += 5 * keys * min(256, q_rows) * 4
    if scratch_bytes > 58 * 2**20 or n_pool != 2 or n_pb % 2 or n_ka != 4:
        return plain_shards(tokens, modality, proj_weight, out_grad)
    offsets, count = {}, 0
    for name, size in (
        ("tok_ka", 2 * n_ka), ("tok_fw", 2 * n_ka), ("mod", n_pb), ("xt_z", n_pb), ("xt_ka", n_ka),
        ("xt_fw", n_ka), ("pj", n_ka), ("kv_z", n_pb * n_ka), ("kv_fw", n_pb * n_ka), ("dk_p", n_pb), ("dk_z", n_pb),
        ("dq_p", n_pb), ("dq_z", n_pb), ("gk_p", n_pb), ("gk_z", n_pb), ("bk_p", n_c),
        ("kar", 4 * n_c), ("rel", 2 * n_c),
    ):
        offsets[name] = count
        count += size
    dims = (n_pb, n_ka, rows, half, group, hd, q_rows, offsets)
    in_vmem = pl.BlockSpec(memory_space=pltpu.VMEM)
    kinds = jnp.broadcast_to(modality.astype(BF16)[:, None], (q_rows, hd))
    made = pl.pallas_call(
        functools.partial(fused, dims),
        out_shape=(
            jax.ShapeDtypeStruct((rows, half), BF16),
            jax.ShapeDtypeStruct((1, slice_rows, group), F32),
        ),
        in_specs=[in_vmem, in_vmem, pl.BlockSpec(memory_space=pl.ANY), in_vmem],
        out_specs=(in_vmem, pl.BlockSpec(memory_space=pl.ANY)),
        scratch_shapes=vmem
        + [
            pltpu.SemaphoreType.DMA,
            pltpu.SemaphoreType.DMA,
            pltpu.SemaphoreType.DMA((count,)),
            pltpu.SemaphoreType.DMA((count,)),
        ],
        compiler_params=pltpu.CompilerParams(
            collective_id=0, has_side_effects=True, vmem_limit_bytes=62 * 2**20
        ),
    )(tokens, kinds, proj_weight, out_grad)
    any_space = pl.BlockSpec(memory_space=pl.ANY)
    return pl.pallas_call(
        hand_over,
        out_shape=tuple(jax.ShapeDtypeStruct(x.shape, x.dtype) for x in made),
        in_specs=[any_space, any_space],
        out_specs=(any_space, any_space),
        scratch_shapes=[pltpu.SemaphoreType.DMA((8,))],
        compiler_params=pltpu.CompilerParams(vmem_limit_bytes=62 * 2**20),
    )(*made)


def solution(mesh):
    return jax.shard_map(
        shards,
        mesh=mesh,
        in_specs=(P(("pb", "ka"), "pool"), P("pb"), P("pool", None, "ka"), P("pool", "pb", "ka")),
        out_specs=(P(("pb", "ka"), "pool"), P("pool", "pb", "ka")),
        check_vma=False,
    )
```

```python
import functools
import math

import jax
import jax.numpy as jnp
from jax import lax
from jax.experimental import pallas as pl
from jax.experimental.pallas import tpu as pltpu
from jax.sharding import PartitionSpec as P


def plain_shards(tokens, modality, proj_weight, out_grad):
    contract_one = (((1,), (1,)), ((), ()))
    contract_zero = (((0,), (0,)), ((), ()))
    pool_index = lax.axis_index("pool")
    pool_count = lax.axis_size("pool")
    head_size = out_grad.shape[2]
    scaling = 1.0 / math.sqrt(head_size)
    token_count = tokens.shape[0]
    half_width = tokens.shape[1]
    group_width = proj_weight.shape[2]
    weight = proj_weight[0].reshape(pool_count, half_width, group_width)
    gathered = lax.all_gather(tokens[None], ("pool", "ka"), axis=0, tiled=True)
    query_count = gathered.shape[0] // pool_count * token_count
    block_tokens = gathered.reshape(pool_count, query_count, half_width)
    owned = (modality == pool_index)[:, None]
    local_proj = jnp.where(
        owned,
        lax.dot_general(
            block_tokens, weight, (((0, 2), (0, 1)), ((), ())), preferred_element_type=jnp.float32
        ),
        0.0,
    )
    projected = lax.psum(local_proj.astype(jnp.bfloat16), "pool")
    queries = lax.dynamic_slice_in_dim(projected, pool_index * head_size, head_size, 1)
    half_rows = query_count // pool_count
    own_keys = projected[:, group_width - 2 * head_size :].reshape(
        pool_count, half_rows, 2 * head_size
    )
    key_value = lax.all_gather(own_keys, "pb", axis=1, tiled=True).reshape(-1, 2 * head_size)
    key_rows = key_value[:, :head_size]
    value_rows = key_value[:, head_size:]
    cotangent = out_grad[0]
    tile_rows = min(512, query_count)
    tile_count = query_count // tile_rows
    q_tiles = queries.reshape(tile_count, tile_rows, head_size)
    o_tiles = cotangent.reshape(tile_count, tile_rows, head_size)

    def advance(running, tile_in):
        q_tile, o_tile = tile_in
        scores = (
            lax.dot_general(q_tile, key_rows, contract_one, preferred_element_type=jnp.float32)
            * scaling
        )
        row_max = jnp.max(scores, axis=1, keepdims=True)
        log_total = row_max + jnp.log(jnp.sum(jnp.exp(scores - row_max), axis=1, keepdims=True))
        softmax = jnp.exp(scores - log_total)
        grad_prob = lax.dot_general(
            o_tile, value_rows, contract_one, preferred_element_type=jnp.float32
        )
        delta = jnp.sum(softmax * grad_prob, axis=1, keepdims=True)
        grad_score = (softmax * (grad_prob - delta)).astype(jnp.bfloat16)
        grad_query = jnp.dot(grad_score, key_rows, preferred_element_type=jnp.float32) * scaling
        new_keys = (
            running[0]
            + lax.dot_general(grad_score, q_tile, contract_zero, preferred_element_type=jnp.float32)
            * scaling
        )
        new_values = running[1] + lax.dot_general(
            softmax.astype(jnp.bfloat16), o_tile, contract_zero, preferred_element_type=jnp.float32
        )
        return ((new_keys, new_values), grad_query)

    key_count = key_rows.shape[0]
    start_state = (
        jnp.zeros((key_count, head_size), jnp.float32),
        jnp.zeros((key_count, head_size), jnp.float32),
    )
    (grad_keys, grad_values), grad_query = lax.scan(advance, start_state, (q_tiles, o_tiles))
    key_terms = jnp.concatenate([grad_keys, grad_values], axis=1)
    key_cell = lax.psum_scatter(
        key_terms.astype(jnp.bfloat16), ("pool", "pb"), scatter_dimension=0, tiled=True
    )
    query_low = grad_query.reshape(query_count, head_size).astype(jnp.bfloat16)
    both_queries, key_block = (
        lax.all_gather(query_low, "pool", axis=1, tiled=True),
        lax.all_gather(key_cell, "pool", axis=0, tiled=True),
    )
    grad_proj = jnp.concatenate([both_queries, key_block], axis=1)
    masked = jnp.where(owned, grad_proj, jnp.zeros_like(grad_proj))
    back = jnp.einsum("rj,pcj->prc", masked, weight, preferred_element_type=jnp.float32)
    stacked = back.reshape(pool_count * (query_count // token_count), token_count, half_width)
    token_sum = lax.psum_scatter(
        stacked.astype(jnp.bfloat16), ("pool", "ka"), scatter_dimension=0, tiled=True
    ).astype(jnp.float32)[0]
    grad_tokens = token_sum.astype(jnp.bfloat16)
    term = jnp.einsum(
        "prc,rj->pcj", block_tokens, masked, preferred_element_type=jnp.float32
    ).reshape(-1, group_width)
    grad_weight = lax.psum_scatter(
        term.astype(jnp.bfloat16), "pb", scatter_dimension=0, tiled=True
    ).astype(jnp.float32)
    return (grad_tokens, grad_weight[None])


BF16 = jnp.bfloat16
F32 = jnp.float32
NT = (((1,), (1,)), ((), ()))


def divisor(total, unit, most):
    best = unit
    for size in range(unit, most + 1, unit):
        if total % size == 0:
            best = size
    return best


def fused(
    dims, tok, mod, weight_hbm, cot, out_tok, out_weight,
    tokbuf, wbuf, xtbuf, modbuf, projloc, projrecv, qbuf, kvbuf, ktbuf, prob, score,
    dkv, dkvp, dkvs, dkvr, gp, mgp, bsend, brecv, bsum, kar, rel, xt, wout, load_sem, store_sem, ss, rs,
):
    n_pb, n_ka, rows, half, group, hd, q_rows, offsets = dims
    scaling = 1.0 / math.sqrt(hd)
    p, b, k = lax.axis_index("pool"), lax.axis_index("pb"), lax.axis_index("ka")
    other = 1 - p
    q_half = q_rows // 2
    hp = n_pb // 2
    n_c, chunk = bsend.shape[0], bsend.shape[2]
    slice_rows = xtbuf.shape[1]
    part = rows // 2
    low, high_bit = lax.rem(k, 2), lax.div(k, 2)
    near = [
        k,
        2 * high_bit + 1 - low,
        2 * (1 - high_bit) + low,
        2 * (1 - high_bit) + 1 - low,
    ]
    kv_at = group - 2 * hd
    partner = (other, b, k)
    sends = []

    def pb_dev(d):
        return (p, lax.rem(b + d, n_pb), k)

    def ka_dev(d):
        return (p, b, lax.rem(k + d, n_ka))

    def b_from(d):
        return lax.rem(b - d + n_pb, n_pb)

    def k_from(d):
        return lax.rem(k - d + n_ka, n_ka)

    def remote(src, dst, name, i, dev):
        at = offsets[name] + i
        return pltpu.make_async_remote_copy(
            src_ref=src, dst_ref=dst, send_sem=ss.at[at], recv_sem=rs.at[at],
            device_id=dev, device_id_type=pl.DeviceIdType.MESH,
        )

    def send(src, dst, name, i, dev):
        copy = remote(src, dst, name, i, dev)
        copy.start()
        sends.append(copy)

    def arrived(dst, name, i):
        remote(dst, dst, name, i, partner).wait_recv()

    def ka_rows(index):
        return pl.ds(pl.multiple_of(index * rows, rows), rows)

    barrier = pltpu.get_barrier_semaphore()
    devs = [partner] + [pb_dev(d) for d in range(1, n_pb)] + [ka_dev(d) for d in range(1, n_ka)]
    for dev in devs:
        pl.semaphore_signal(barrier, inc=1, device_id=dev, device_id_type=pl.DeviceIdType.MESH)
    load = pltpu.make_async_copy(weight_hbm.at[0], wbuf, load_sem)
    load.start()
    pl.semaphore_wait(barrier, len(devs))

    def tok_part(pool, slot, h):
        return tokbuf.at[pool, pl.ds(slot * rows + h * part, part)]

    for e, h in ((1, 0), (2, 1), (1, 1), (2, 0)):
        send(
            tok.at[pl.ds(h * part, part)], tok_part(p, e, h), "tok_ka", 2 * e + h, (p, b, near[e])
        )
    for h in range(2):
        send(tok.at[pl.ds(h * part, part)], tok_part(p, 0, h), "tok_fw", h, partner)
    for d in range(1, n_pb):
        send(mod, modbuf.at[b], "mod", d, pb_dev(d))
    tokbuf[p, :rows, :] = tok[...]
    modbuf[b] = mod[...]

    for i in range(half // 128):
        cols = slice(i * 128, (i + 1) * 128)
        xt[cols, :] = jnp.transpose(tok[:, cols].astype(F32)).astype(BF16)

    def xt_part(target):
        return pl.ds(pl.multiple_of(lax.rem(target, hp) * slice_rows, 16), slice_rows)

    mine = lax.div(b, hp) == p
    for d in range(1, n_pb):
        target = lax.rem(b + d, n_pb)

        @pl.when(lax.div(target, hp) == p)
        def _(d=d, target=target):
            remote(
                xt.at[xt_part(target)], xtbuf.at[b, :, ka_rows(k)], "xt_z", d, pb_dev(d)
            ).start()

    @pl.when(mine)
    def _():
        xtbuf[b, :, ka_rows(k)] = xt[xt_part(b), :]

    def own_mask(index):
        return modbuf[index].astype(F32)[:, :1] == p.astype(F32)

    def hand_on(e, h, relay_to):
        region = tok_part(p, e, h)
        arrived(region, "tok_ka", 2 * e + h)
        if relay_to is not None:
            send(region, tok_part(p, 3, h), "tok_ka", 6 + h, (p, b, near[relay_to]))
        send(region, region, "tok_fw", 2 * e + h, partner)

    arrivals = {}

    def project(e, count):
        for slot in range(e, e + count):
            for h in range(2):
                arrived(tok_part(other, slot, h), "tok_fw", 2 * slot + h)
        at = pl.ds(e * rows, count * rows)
        proj = jnp.dot(tokbuf[0, at, :], wbuf[:half], preferred_element_type=F32)
        proj += jnp.dot(tokbuf[1, at, :], wbuf[half:], preferred_element_type=F32)
        projloc[at, :] = proj.astype(BF16)
        send(projloc.at[at], projrecv.at[at], "pj", e, partner)
        arrivals[e] = at

    def settle(e):
        at = ka_rows(near[e])
        slot = pl.ds(e * rows, rows)
        if e in arrivals:
            arrived(projrecv.at[arrivals[e]], "pj", e)
        owned = modbuf[b, at, :].astype(F32)[:, :1] == p.astype(F32)
        projected = jnp.where(owned, projloc[slot, :].astype(F32), projrecv[slot, :].astype(F32))
        qbuf[at, :] = jnp.where(p == 0, projected[:, :hd], projected[:, hd : 2 * hd]).astype(BF16)
        kvbuf[b, near[e]] = projected[:, kv_at:].astype(BF16).reshape(2, part, 2 * hd)
        region = kvbuf.at[b, near[e], p]
        for d in range(1, n_pb):
            send(region, region, "kv_z", d * n_ka + e, pb_dev(d))

    def pass_keys(e):
        for d in range(1, n_pb):
            region = kvbuf.at[b_from(d), near[e], p]
            arrived(region, "kv_z", d * n_ka + e)
            send(region, region, "kv_fw", d * n_ka + e, partner)

    load.wait()
    project(0, 1)
    hand_on(1, 0, 2)
    hand_on(2, 1, 1)
    settle(0)
    hand_on(1, 1, None)
    hand_on(2, 0, None)
    project(1, 2)
    settle(1)
    settle(2)
    pass_keys(0)
    hand_on(3, 0, None)
    hand_on(3, 1, None)
    project(3, 1)

    @pl.when(mine)
    def _():
        for d in range(1, n_pb):
            arrived(xtbuf.at[b_from(d), :, ka_rows(k)], "xt_z", d)
        for d in range(1, n_ka):
            region = xtbuf.at[:, :, ka_rows(k)]
            remote(region, region, "xt_ka", d, ka_dev(d)).start()
        region = xtbuf.at[:, :, ka_rows(k)]
        remote(region, region, "xt_fw", 0, partner).start()

    settle(3)
    for e in range(1, n_ka):
        pass_keys(e)
    for e in range(n_ka):
        for d in range(1, n_pb):
            arrived(kvbuf.at[b_from(d), near[e], other], "kv_fw", d * n_ka + e)

    keys = n_pb * q_rows
    key_rows = kvbuf[:, :, :, :, :hd].reshape(keys, hd)
    ktbuf[...] = jnp.transpose(key_rows.astype(F32)).astype(BF16)
    tile = min(256, q_rows)
    for t in range(q_rows // tile):
        at = slice(t * tile, (t + 1) * tile)
        key_rows = kvbuf[:, :, :, :, :hd].reshape(keys, hd)
        value_rows = kvbuf[:, :, :, :, hd:].reshape(keys, hd)
        scores = lax.dot_general(key_rows, qbuf[at, :], NT, preferred_element_type=F32)
        high = jnp.max(scores, axis=0, keepdims=True)
        raised = jnp.exp((scores - high) * scaling)
        softmax = raised * (1.0 / jnp.sum(raised, axis=0, keepdims=True))
        grad_prob = lax.dot_general(value_rows, cot[0, at, :], NT, preferred_element_type=F32)
        delta = jnp.sum(softmax * grad_prob, axis=0, keepdims=True)
        grad_score = (softmax * (grad_prob - delta)).astype(BF16)
        prob[:, :, at] = softmax.astype(BF16).reshape(n_pb, q_rows, tile)
        score[:, :, at] = grad_score.reshape(n_pb, q_rows, tile)

    def key_block(d):
        block = lax.rem(b + d, n_pb)
        dk = jnp.dot(score[block], qbuf[...], preferred_element_type=F32) * scaling
        dv = jnp.dot(prob[block], cot[0], preferred_element_type=F32)
        dkv[block, :, :, :hd] = dk.astype(BF16).reshape(2, q_half, hd)
        dkv[block, :, :, hd:] = dv.astype(BF16).reshape(2, q_half, hd)
        send(dkv.at[block, other], dkvp.at[block], "dk_p", d, partner)

    def key_sum(d):
        block = lax.rem(b + d, n_pb)
        arrived(dkvp.at[block], "dk_p", d)
        dkvs[block] = (dkv[block, p].astype(F32) + dkvp[block].astype(F32)).astype(BF16)
        if d:
            send(dkvs.at[block], dkvr.at[d], "dk_z", d, pb_dev(d))

    turns = list(range(1, n_pb)) + [0]
    for i, d in enumerate(turns):
        key_block(d)
        if i:
            key_sum(turns[i - 1])
    key_sum(0)
    dq = jnp.dot(ktbuf[...], score[...].reshape(keys, q_rows), preferred_element_type=F32) * scaling
    dq = jnp.transpose(dq).astype(BF16)

    @pl.when(p == 0)
    def _():
        gp[b, :, :hd] = dq

    @pl.when(p == 1)
    def _():
        gp[b, :, hd : 2 * hd] = dq

    def q_cols(pool):
        return pl.ds(pl.multiple_of(pool * hd, hd), hd)

    def half_rows(pool):
        return pl.ds(pl.multiple_of(pool * q_half, q_half), q_half)

    dq_own = gp.at[b, :, q_cols(p)]
    send(dq_own, dq_own, "dq_p", 0, partner)
    for d in range(1, n_pb):
        send(dq_own, dq_own, "dq_z", d, pb_dev(d))

    total = dkvs[b].astype(F32)
    for d in range(1, n_pb):
        arrived(dkvr.at[d], "dk_z", d)
        total += dkvr[d].astype(F32)
    gp[b, half_rows(p), kv_at:] = total.astype(BF16)
    kv_own = gp.at[b, half_rows(p), pl.ds(kv_at, 2 * hd)]
    send(kv_own, kv_own, "gk_p", 0, partner)
    for d in range(1, n_pb):
        send(kv_own, kv_own, "gk_z", d, pb_dev(d))
    arrived(gp.at[b, :, q_cols(other)], "dq_p", 0)
    arrived(gp.at[b, half_rows(other), pl.ds(kv_at, 2 * hd)], "gk_p", 0)

    mgp[b] = jnp.where(own_mask(b), gp[b].astype(F32), 0.0).astype(BF16)

    def relayed(e, c):
        h = 2 - e
        arrived(rel.at[h, c], "rel", h * n_c + c)
        at = pl.ds(pl.multiple_of(near[e] * rows + h * part, part), part)
        bsum[c, at, :] = (bsum[c, at, :].astype(F32) + rel[h, c].astype(F32)).astype(BF16)
        return partial_copy(e, h, c)

    def partial_copy(e, h, c):
        at = pl.ds(pl.multiple_of(near[e] * rows + h * part, part), part)
        return remote(
            bsum.at[c, at], kar.at[e - 1, c, pl.ds(h * part, part)],
            "kar", (2 * (e - 1) + h) * n_c + c, (p, b, near[e]),
        )

    def relay_copy(h, c):
        at = pl.ds(pl.multiple_of(near[3] * rows + h * part, part), part)
        return remote(bsum.at[c, at], rel.at[h, c], "rel", h * n_c + c, (p, b, near[1 + h]))

    def back_chunk(c, carry):
        def product(pool):
            at = pl.ds(pl.multiple_of(pool * half + c * chunk, 128), chunk)
            return lax.dot_general(mgp[b], wbuf[at, :], NT, preferred_element_type=F32)

        bsend[c] = product(other).astype(BF16)
        remote(bsend.at[c], brecv.at[c], "bk_p", c, partner).start()
        bsum[c] = product(p).astype(BF16)

        @pl.when(c > 0)
        def _():
            pool_sum(c - 1)

        return carry

    def pool_sum(c):
        arrived(brecv.at[c], "bk_p", c)
        bsum[c] = (bsum[c].astype(F32) + brecv[c].astype(F32)).astype(BF16)
        for h in range(2):
            relay_copy(h, c).start()
        partial_copy(1, 0, c).start()
        partial_copy(2, 1, c).start()

    def relay_sums(c):
        for e in (2, 1):
            relayed(e, c).start()

    lax.fori_loop(0, n_c, back_chunk, 0)
    pool_sum(n_c - 1)
    @pl.when(mine)
    def _():
        for d in range(1, n_ka):
            region = xtbuf.at[:, :, ka_rows(k_from(d))]
            arrived(region, "xt_ka", d)
            remote(region, region, "xt_fw", d, partner).start()

    early = min(3, n_c)
    for c in range(early):
        relay_sums(c)

    for d in range(1, n_pb):
        region = gp.at[b_from(d), :, q_cols(p)]
        arrived(region, "dq_z", d)
        send(region, region, "dq_p", d, partner)
    for d in range(1, n_pb):
        region = gp.at[b_from(d), half_rows(p), pl.ds(kv_at, 2 * hd)]
        arrived(region, "gk_z", d)
        send(region, region, "gk_p", d, partner)
    for d in range(1, n_pb):
        arrived(modbuf.at[b_from(d)], "mod", d)
    for d in range(1, n_pb):
        arrived(gp.at[b_from(d), :, q_cols(other)], "dq_p", d)
        arrived(gp.at[b_from(d), half_rows(other), pl.ds(kv_at, 2 * hd)], "gk_p", d)
        source = b_from(d)
        mgp[source] = jnp.where(own_mask(source), gp[source].astype(F32), 0.0).astype(BF16)

    @pl.when(jnp.logical_not(mine))
    def _():
        for d in range(n_ka):
            arrived(xtbuf.at[:, :, ka_rows(k_from(d))], "xt_fw", d)

    tiles = max(t for t in range(1, 7) if slice_rows % (16 * t) == 0)
    w_tile = slice_rows // tiles

    def weight_rows(t):
        at = pl.ds(pl.multiple_of(t * w_tile, 16), w_tile)
        acc = jnp.dot(xtbuf[0, at, :], mgp[0], preferred_element_type=F32)
        for i in range(1, n_pb):
            acc += jnp.dot(xtbuf[i, at, :], mgp[i], preferred_element_type=F32)
        wout[at, :] = acc

    def weight_and_relay(t, carry):
        weight_rows(t)

        @pl.when(t + early < n_c)
        def _():
            relay_sums(t + early)

        return carry

    lax.fori_loop(0, tiles, weight_and_relay, 0)
    for c in range(early + tiles, n_c):
        relay_sums(c)
    store = pltpu.make_async_copy(wout, out_weight.at[0], store_sem)
    store.start()

    for c in range(n_c):
        acc = bsum[c, ka_rows(k), :].astype(F32)
        for e in (1, 2):
            for h in range(2):
                arrived(kar.at[e - 1, c, pl.ds(h * part, part)], "kar", (2 * (e - 1) + h) * n_c + c)
            acc += kar[e - 1, c].astype(F32)
        out_tok[:, c * chunk : (c + 1) * chunk] = acc.astype(BF16)

    store.wait()
    for copy in sends:
        copy.wait_send()
    for d in range(1, n_pb):
        target = lax.rem(b + d, n_pb)

        @pl.when(lax.div(target, hp) == p)
        def _(d=d, target=target):
            remote(xt.at[xt_part(target)], xtbuf.at[b, :, ka_rows(k)], "xt_z", d, pb_dev(d)).wait_send()

    @pl.when(mine)
    def _():
        region = xtbuf.at[:, :, ka_rows(k)]
        for d in range(1, n_ka):
            remote(region, region, "xt_ka", d, ka_dev(d)).wait_send()
        for d in range(n_ka):
            region = xtbuf.at[:, :, ka_rows(k_from(d))]
            remote(region, region, "xt_fw", d, partner).wait_send()

    def sent(c, carry):
        remote(bsend.at[c], brecv.at[c], "bk_p", c, partner).wait_send()
        for h in range(2):
            relay_copy(h, c).wait_send()
            for e in (1, 2):
                partial_copy(e, h, c).wait_send()
        return carry

    lax.fori_loop(0, n_c, sent, 0)


def hand_over(tok_from, weight_from, tok_to, weight_to, tok_mid, weight_mid, in_sems, out_sems):
    count = in_sems.shape[0]
    pieces = []
    for source, middle, target, first, parts in (
        (weight_from.at[0], weight_mid, weight_to.at[0], 0, count - 1),
        (tok_from, tok_mid, tok_to, count - 1, 1),
    ):
        if source.shape[0] % (16 * parts):
            parts = 1
        rows = source.shape[0] // parts
        for i in range(parts):
            at = pl.ds(i * rows, rows)
            pieces.append(
                (
                    pltpu.make_async_copy(source.at[at], middle.at[at], in_sems.at[first + i]),
                    pltpu.make_async_copy(middle.at[at], target.at[at], out_sems.at[first + i]),
                )
            )
    for read, _ in pieces:
        read.start()
    for read, write in pieces:
        read.wait()
        write.start()
    for _, write in pieces:
        write.wait()


def shards(tokens, modality, proj_weight, out_grad):
    n_pool, n_pb, n_ka = (lax.axis_size(name) for name in ("pool", "pb", "ka"))
    rows, half = tokens.shape
    group = proj_weight.shape[2]
    width = proj_weight.shape[1]
    q_rows, hd = out_grad.shape[1:]
    keys = n_pb * q_rows
    slice_rows = width // n_pb
    chunk = divisor(half, 128, 512)
    n_c = half // chunk
    vmem, scratch_bytes = [], 0
    shapes = [
        ((2, q_rows, half), BF16), ((width, group), BF16), ((n_pb, slice_rows, q_rows), BF16),
        ((n_pb, q_rows, hd), BF16), ((q_rows, group), BF16), ((q_rows, group), BF16),
        ((q_rows, hd), BF16), ((n_pb, n_ka, 2, rows // 2, 2 * hd), BF16), ((hd, keys), BF16),
        ((n_pb, q_rows, q_rows), BF16), ((n_pb, q_rows, q_rows), BF16), ((n_pb, 2, q_rows // 2, 2 * hd), BF16),
        ((n_pb, q_rows // 2, 2 * hd), BF16), ((n_pb, q_rows // 2, 2 * hd), BF16),
        ((n_pb, q_rows // 2, 2 * hd), BF16), ((n_pb, q_rows, group), BF16),
        ((n_pb, q_rows, group), BF16), ((n_c, q_rows, chunk), BF16), ((n_c, q_rows, chunk), BF16),
        ((n_c, q_rows, chunk), BF16), ((2, n_c, rows, chunk), BF16),
        ((2, n_c, rows // 2, chunk), BF16), ((half, rows), BF16), ((slice_rows, group), F32),
    ]
    for shape, kind in shapes:
        vmem.append(pltpu.VMEM(shape, kind))
        scratch_bytes += math.prod(shape) * jnp.dtype(kind).itemsize
    scratch_bytes += 5 * keys * min(256, q_rows) * 4
    if scratch_bytes > 58 * 2**20 or n_pool != 2 or n_pb % 2 or n_ka != 4:
        return plain_shards(tokens, modality, proj_weight, out_grad)
    offsets, count = {}, 0
    for name, size in (
        ("tok_ka", 2 * n_ka), ("tok_fw", 2 * n_ka), ("mod", n_pb), ("xt_z", n_pb), ("xt_ka", n_ka),
        ("xt_fw", n_ka), ("pj", n_ka), ("kv_z", n_pb * n_ka), ("kv_fw", n_pb * n_ka), ("dk_p", n_pb), ("dk_z", n_pb),
        ("dq_p", n_pb), ("dq_z", n_pb), ("gk_p", n_pb), ("gk_z", n_pb), ("bk_p", n_c),
        ("kar", 4 * n_c), ("rel", 2 * n_c),
    ):
        offsets[name] = count
        count += size
    dims = (n_pb, n_ka, rows, half, group, hd, q_rows, offsets)
    in_vmem = pl.BlockSpec(memory_space=pltpu.VMEM)
    kinds = jnp.broadcast_to(modality.astype(BF16)[:, None], (q_rows, hd))
    made = pl.pallas_call(
        functools.partial(fused, dims),
        out_shape=(
            jax.ShapeDtypeStruct((rows, half), BF16),
            jax.ShapeDtypeStruct((1, slice_rows, group), F32),
        ),
        in_specs=[in_vmem, in_vmem, pl.BlockSpec(memory_space=pl.ANY), in_vmem],
        out_specs=(in_vmem, pl.BlockSpec(memory_space=pl.ANY)),
        scratch_shapes=vmem
        + [
            pltpu.SemaphoreType.DMA,
            pltpu.SemaphoreType.DMA,
            pltpu.SemaphoreType.DMA((count,)),
            pltpu.SemaphoreType.DMA((count,)),
        ],
        compiler_params=pltpu.CompilerParams(
            collective_id=0, has_side_effects=True, vmem_limit_bytes=62 * 2**20
        ),
    )(tokens, kinds, proj_weight, out_grad)
    any_space = pl.BlockSpec(memory_space=pl.ANY)
    return pl.pallas_call(
        hand_over,
        out_shape=tuple(jax.ShapeDtypeStruct(x.shape, x.dtype) for x in made),
        in_specs=[any_space, any_space],
        out_specs=(any_space, any_space),
        scratch_shapes=[
            pltpu.VMEM(made[0].shape, made[0].dtype),
            pltpu.VMEM(made[1].shape[1:], made[1].dtype),
            pltpu.SemaphoreType.DMA((5,)),
            pltpu.SemaphoreType.DMA((5,)),
        ],
        compiler_params=pltpu.CompilerParams(vmem_limit_bytes=62 * 2**20),
    )(*made)


def solution(mesh):
    return jax.shard_map(
        shards,
        mesh=mesh,
        in_specs=(P(("pb", "ka"), "pool"), P("pb"), P("pool", None, "ka"), P("pool", "pb", "ka")),
        out_specs=(P(("pb", "ka"), "pool"), P("pool", "pb", "ka")),
        check_vma=False,
    )
```

```python
import functools
import math

import jax
import jax.numpy as jnp
from jax import lax
from jax.experimental import pallas as pl
from jax.experimental.pallas import tpu as pltpu
from jax.sharding import PartitionSpec as P


def plain_shards(tokens, modality, proj_weight, out_grad):
    contract_one = (((1,), (1,)), ((), ()))
    contract_zero = (((0,), (0,)), ((), ()))
    pool_index = lax.axis_index("pool")
    pool_count = lax.axis_size("pool")
    head_size = out_grad.shape[2]
    scaling = 1.0 / math.sqrt(head_size)
    token_count = tokens.shape[0]
    half_width = tokens.shape[1]
    group_width = proj_weight.shape[2]
    weight = proj_weight[0].reshape(pool_count, half_width, group_width)
    gathered = lax.all_gather(tokens[None], ("pool", "ka"), axis=0, tiled=True)
    query_count = gathered.shape[0] // pool_count * token_count
    block_tokens = gathered.reshape(pool_count, query_count, half_width)
    owned = (modality == pool_index)[:, None]
    local_proj = jnp.where(
        owned,
        lax.dot_general(
            block_tokens, weight, (((0, 2), (0, 1)), ((), ())), preferred_element_type=jnp.float32
        ),
        0.0,
    )
    projected = lax.psum(local_proj.astype(jnp.bfloat16), "pool")
    queries = lax.dynamic_slice_in_dim(projected, pool_index * head_size, head_size, 1)
    half_rows = query_count // pool_count
    own_keys = projected[:, group_width - 2 * head_size :].reshape(
        pool_count, half_rows, 2 * head_size
    )
    key_value = lax.all_gather(own_keys, "pb", axis=1, tiled=True).reshape(-1, 2 * head_size)
    key_rows = key_value[:, :head_size]
    value_rows = key_value[:, head_size:]
    cotangent = out_grad[0]
    tile_rows = min(512, query_count)
    tile_count = query_count // tile_rows
    q_tiles = queries.reshape(tile_count, tile_rows, head_size)
    o_tiles = cotangent.reshape(tile_count, tile_rows, head_size)

    def advance(running, tile_in):
        q_tile, o_tile = tile_in
        scores = (
            lax.dot_general(q_tile, key_rows, contract_one, preferred_element_type=jnp.float32)
            * scaling
        )
        row_max = jnp.max(scores, axis=1, keepdims=True)
        log_total = row_max + jnp.log(jnp.sum(jnp.exp(scores - row_max), axis=1, keepdims=True))
        softmax = jnp.exp(scores - log_total)
        grad_prob = lax.dot_general(
            o_tile, value_rows, contract_one, preferred_element_type=jnp.float32
        )
        delta = jnp.sum(softmax * grad_prob, axis=1, keepdims=True)
        grad_score = (softmax * (grad_prob - delta)).astype(jnp.bfloat16)
        grad_query = jnp.dot(grad_score, key_rows, preferred_element_type=jnp.float32) * scaling
        new_keys = (
            running[0]
            + lax.dot_general(grad_score, q_tile, contract_zero, preferred_element_type=jnp.float32)
            * scaling
        )
        new_values = running[1] + lax.dot_general(
            softmax.astype(jnp.bfloat16), o_tile, contract_zero, preferred_element_type=jnp.float32
        )
        return ((new_keys, new_values), grad_query)

    key_count = key_rows.shape[0]
    start_state = (
        jnp.zeros((key_count, head_size), jnp.float32),
        jnp.zeros((key_count, head_size), jnp.float32),
    )
    (grad_keys, grad_values), grad_query = lax.scan(advance, start_state, (q_tiles, o_tiles))
    key_terms = jnp.concatenate([grad_keys, grad_values], axis=1)
    key_cell = lax.psum_scatter(
        key_terms.astype(jnp.bfloat16), ("pool", "pb"), scatter_dimension=0, tiled=True
    )
    query_low = grad_query.reshape(query_count, head_size).astype(jnp.bfloat16)
    both_queries, key_block = (
        lax.all_gather(query_low, "pool", axis=1, tiled=True),
        lax.all_gather(key_cell, "pool", axis=0, tiled=True),
    )
    grad_proj = jnp.concatenate([both_queries, key_block], axis=1)
    masked = jnp.where(owned, grad_proj, jnp.zeros_like(grad_proj))
    back = jnp.einsum("rj,pcj->prc", masked, weight, preferred_element_type=jnp.float32)
    stacked = back.reshape(pool_count * (query_count // token_count), token_count, half_width)
    token_sum = lax.psum_scatter(
        stacked.astype(jnp.bfloat16), ("pool", "ka"), scatter_dimension=0, tiled=True
    ).astype(jnp.float32)[0]
    grad_tokens = token_sum.astype(jnp.bfloat16)
    term = jnp.einsum(
        "prc,rj->pcj", block_tokens, masked, preferred_element_type=jnp.float32
    ).reshape(-1, group_width)
    grad_weight = lax.psum_scatter(
        term.astype(jnp.bfloat16), "pb", scatter_dimension=0, tiled=True
    ).astype(jnp.float32)
    return (grad_tokens, grad_weight[None])


BF16 = jnp.bfloat16
F32 = jnp.float32
NT = (((1,), (1,)), ((), ()))


def divisor(total, unit, most):
    best = unit
    for size in range(unit, most + 1, unit):
        if total % size == 0:
            best = size
    return best


def fused(
    dims, tok, mod, weight_hbm, cot, out_tok, out_weight,
    tokbuf, wbuf, xtbuf, modbuf, projloc, projrecv, qbuf, kvbuf, ktbuf, prob, score,
    dkv, dkvp, dkvs, dkvr, gp, mgp, bsend, brecv, bsum, kar, rel, xt, wout, load_sem, store_sem, ss, rs,
):
    n_pb, n_ka, rows, half, group, hd, q_rows, offsets = dims
    scaling = 1.0 / math.sqrt(hd)
    p, b, k = lax.axis_index("pool"), lax.axis_index("pb"), lax.axis_index("ka")
    other = 1 - p
    q_half = q_rows // 2
    hp = n_pb // 2
    n_c, chunk = bsend.shape[0], bsend.shape[2]
    slice_rows = xtbuf.shape[1]
    part = rows // 2
    low, high_bit = lax.rem(k, 2), lax.div(k, 2)
    near = [
        k,
        2 * high_bit + 1 - low,
        2 * (1 - high_bit) + low,
        2 * (1 - high_bit) + 1 - low,
    ]
    kv_at = group - 2 * hd
    partner = (other, b, k)
    sends = []

    def pb_dev(d):
        return (p, lax.rem(b + d, n_pb), k)

    def ka_dev(d):
        return (p, b, lax.rem(k + d, n_ka))

    def b_from(d):
        return lax.rem(b - d + n_pb, n_pb)

    def k_from(d):
        return lax.rem(k - d + n_ka, n_ka)

    def remote(src, dst, name, i, dev):
        at = offsets[name] + i
        return pltpu.make_async_remote_copy(
            src_ref=src, dst_ref=dst, send_sem=ss.at[at], recv_sem=rs.at[at],
            device_id=dev, device_id_type=pl.DeviceIdType.MESH,
        )

    def send(src, dst, name, i, dev):
        copy = remote(src, dst, name, i, dev)
        copy.start()
        sends.append(copy)

    def arrived(dst, name, i):
        remote(dst, dst, name, i, partner).wait_recv()

    def ka_rows(index):
        return pl.ds(pl.multiple_of(index * rows, rows), rows)

    barrier = pltpu.get_barrier_semaphore()
    devs = [partner] + [pb_dev(d) for d in range(1, n_pb)] + [ka_dev(d) for d in range(1, n_ka)]
    for dev in devs:
        pl.semaphore_signal(barrier, inc=1, device_id=dev, device_id_type=pl.DeviceIdType.MESH)
    load = pltpu.make_async_copy(weight_hbm.at[0], wbuf, load_sem)
    load.start()
    pl.semaphore_wait(barrier, len(devs))

    def tok_part(pool, slot, h):
        return tokbuf.at[pool, pl.ds(slot * rows + h * part, part)]

    for e, h in ((1, 0), (2, 1), (1, 1), (2, 0)):
        send(
            tok.at[pl.ds(h * part, part)], tok_part(p, e, h), "tok_ka", 2 * e + h, (p, b, near[e])
        )
    for h in range(2):
        send(tok.at[pl.ds(h * part, part)], tok_part(p, 0, h), "tok_fw", h, partner)
    for d in range(1, n_pb):
        send(mod, modbuf.at[b], "mod", d, pb_dev(d))
    tokbuf[p, :rows, :] = tok[...]
    modbuf[b] = mod[...]

    for i in range(half // 128):
        cols = slice(i * 128, (i + 1) * 128)
        xt[cols, :] = jnp.transpose(tok[:, cols].astype(F32)).astype(BF16)

    def xt_part(target):
        return pl.ds(pl.multiple_of(lax.rem(target, hp) * slice_rows, 16), slice_rows)

    mine = lax.div(b, hp) == p
    for d in range(1, n_pb):
        target = lax.rem(b + d, n_pb)

        @pl.when(lax.div(target, hp) == p)
        def _(d=d, target=target):
            remote(
                xt.at[xt_part(target)], xtbuf.at[b, :, ka_rows(k)], "xt_z", d, pb_dev(d)
            ).start()

    @pl.when(mine)
    def _():
        xtbuf[b, :, ka_rows(k)] = xt[xt_part(b), :]

    def own_mask(index):
        return modbuf[index].astype(F32)[:, :1] == p.astype(F32)

    def hand_on(e, h, relay_to):
        region = tok_part(p, e, h)
        arrived(region, "tok_ka", 2 * e + h)
        if relay_to is not None:
            send(region, tok_part(p, 3, h), "tok_ka", 6 + h, (p, b, near[relay_to]))
        send(region, region, "tok_fw", 2 * e + h, partner)

    arrivals = {}

    def project(e, count):
        for slot in range(e, e + count):
            for h in range(2):
                arrived(tok_part(other, slot, h), "tok_fw", 2 * slot + h)
        at = pl.ds(e * rows, count * rows)
        proj = jnp.dot(tokbuf[0, at, :], wbuf[:half], preferred_element_type=F32)
        proj += jnp.dot(tokbuf[1, at, :], wbuf[half:], preferred_element_type=F32)
        projloc[at, :] = proj.astype(BF16)
        send(projloc.at[at], projrecv.at[at], "pj", e, partner)
        arrivals[e] = at

    def settle(e):
        at = ka_rows(near[e])
        slot = pl.ds(e * rows, rows)
        if e in arrivals:
            arrived(projrecv.at[arrivals[e]], "pj", e)
        owned = modbuf[b, at, :].astype(F32)[:, :1] == p.astype(F32)
        projected = jnp.where(owned, projloc[slot, :].astype(F32), projrecv[slot, :].astype(F32))
        qbuf[at, :] = jnp.where(p == 0, projected[:, :hd], projected[:, hd : 2 * hd]).astype(BF16)
        kvbuf[b, near[e]] = projected[:, kv_at:].astype(BF16).reshape(2, part, 2 * hd)
        region = kvbuf.at[b, near[e], p]
        for d in range(1, n_pb):
            send(region, region, "kv_z", d * n_ka + e, pb_dev(d))

    def pass_keys(e):
        for d in range(1, n_pb):
            region = kvbuf.at[b_from(d), near[e], p]
            arrived(region, "kv_z", d * n_ka + e)
            send(region, region, "kv_fw", d * n_ka + e, partner)

    load.wait()
    project(0, 1)
    hand_on(1, 0, 2)
    hand_on(2, 1, 1)
    settle(0)
    hand_on(1, 1, None)
    hand_on(2, 0, None)
    project(1, 2)
    settle(1)
    settle(2)
    pass_keys(0)
    hand_on(3, 0, None)
    hand_on(3, 1, None)
    project(3, 1)

    @pl.when(mine)
    def _():
        for d in range(1, n_pb):
            arrived(xtbuf.at[b_from(d), :, ka_rows(k)], "xt_z", d)
        for d in range(1, n_ka):
            region = xtbuf.at[:, :, ka_rows(k)]
            remote(region, region, "xt_ka", d, ka_dev(d)).start()
        region = xtbuf.at[:, :, ka_rows(k)]
        remote(region, region, "xt_fw", 0, partner).start()

    settle(3)
    for e in range(1, n_ka):
        pass_keys(e)
    for e in range(n_ka):
        for d in range(1, n_pb):
            arrived(kvbuf.at[b_from(d), near[e], other], "kv_fw", d * n_ka + e)

    keys = n_pb * q_rows
    tile = min(256, q_rows)
    for t in range(q_rows // tile):
        at = slice(t * tile, (t + 1) * tile)
        key_rows = kvbuf[:, :, :, :, :hd].reshape(keys, hd)
        value_rows = kvbuf[:, :, :, :, hd:].reshape(keys, hd)
        scores = lax.dot_general(key_rows, qbuf[at, :], NT, preferred_element_type=F32)
        high = jnp.max(scores, axis=0, keepdims=True)
        raised = jnp.exp((scores - high) * scaling)
        softmax = raised * (1.0 / jnp.sum(raised, axis=0, keepdims=True))
        grad_prob = lax.dot_general(value_rows, cot[0, at, :], NT, preferred_element_type=F32)
        delta = jnp.sum(softmax * grad_prob, axis=0, keepdims=True)
        grad_score = (softmax * (grad_prob - delta)).astype(BF16)
        prob[:, :, at] = softmax.astype(BF16).reshape(n_pb, q_rows, tile)
        score[:, :, at] = grad_score.reshape(n_pb, q_rows, tile)

    def key_block(d):
        block = lax.rem(b + d, n_pb)
        dk = jnp.dot(score[block], qbuf[...], preferred_element_type=F32) * scaling
        dv = jnp.dot(prob[block], cot[0], preferred_element_type=F32)
        dkv[block, :, :, :hd] = dk.astype(BF16).reshape(2, q_half, hd)
        dkv[block, :, :, hd:] = dv.astype(BF16).reshape(2, q_half, hd)
        send(dkv.at[block, other], dkvp.at[block], "dk_p", d, partner)

    def key_sum(d):
        block = lax.rem(b + d, n_pb)
        arrived(dkvp.at[block], "dk_p", d)
        dkvs[block] = (dkv[block, p].astype(F32) + dkvp[block].astype(F32)).astype(BF16)
        if d:
            send(dkvs.at[block], dkvr.at[d], "dk_z", d, pb_dev(d))

    turns = list(range(1, n_pb)) + [0]
    for i, d in enumerate(turns):
        key_block(d)
        if i:
            key_sum(turns[i - 1])
    key_rows = kvbuf[:, :, :, :, :hd].reshape(keys, hd)
    ktbuf[...] = jnp.transpose(key_rows.astype(F32)).astype(BF16)
    key_sum(0)
    dq = jnp.dot(ktbuf[...], score[...].reshape(keys, q_rows), preferred_element_type=F32) * scaling
    dq = jnp.transpose(dq).astype(BF16)

    @pl.when(p == 0)
    def _():
        gp[b, :, :hd] = dq

    @pl.when(p == 1)
    def _():
        gp[b, :, hd : 2 * hd] = dq

    def q_cols(pool):
        return pl.ds(pl.multiple_of(pool * hd, hd), hd)

    def half_rows(pool):
        return pl.ds(pl.multiple_of(pool * q_half, q_half), q_half)

    dq_own = gp.at[b, :, q_cols(p)]
    send(dq_own, dq_own, "dq_p", 0, partner)
    for d in range(1, n_pb):
        send(dq_own, dq_own, "dq_z", d, pb_dev(d))

    total = dkvs[b].astype(F32)
    for d in range(1, n_pb):
        arrived(dkvr.at[d], "dk_z", d)
        total += dkvr[d].astype(F32)
    gp[b, half_rows(p), kv_at:] = total.astype(BF16)
    kv_own = gp.at[b, half_rows(p), pl.ds(kv_at, 2 * hd)]
    send(kv_own, kv_own, "gk_p", 0, partner)
    for d in range(1, n_pb):
        send(kv_own, kv_own, "gk_z", d, pb_dev(d))
    arrived(gp.at[b, :, q_cols(other)], "dq_p", 0)
    arrived(gp.at[b, half_rows(other), pl.ds(kv_at, 2 * hd)], "gk_p", 0)

    mgp[b] = jnp.where(own_mask(b), gp[b].astype(F32), 0.0).astype(BF16)

    def relayed(e, c):
        h = 2 - e
        arrived(rel.at[h, c], "rel", h * n_c + c)
        at = pl.ds(pl.multiple_of(near[e] * rows + h * part, part), part)
        bsum[c, at, :] = (bsum[c, at, :].astype(F32) + rel[h, c].astype(F32)).astype(BF16)
        return partial_copy(e, h, c)

    def partial_copy(e, h, c):
        at = pl.ds(pl.multiple_of(near[e] * rows + h * part, part), part)
        return remote(
            bsum.at[c, at], kar.at[e - 1, c, pl.ds(h * part, part)],
            "kar", (2 * (e - 1) + h) * n_c + c, (p, b, near[e]),
        )

    def relay_copy(h, c):
        at = pl.ds(pl.multiple_of(near[3] * rows + h * part, part), part)
        return remote(bsum.at[c, at], rel.at[h, c], "rel", h * n_c + c, (p, b, near[1 + h]))

    def back_chunk(c, carry):
        def product(pool):
            at = pl.ds(pl.multiple_of(pool * half + c * chunk, 128), chunk)
            return lax.dot_general(mgp[b], wbuf[at, :], NT, preferred_element_type=F32)

        bsend[c] = product(other).astype(BF16)
        remote(bsend.at[c], brecv.at[c], "bk_p", c, partner).start()
        bsum[c] = product(p).astype(BF16)

        @pl.when(c > 0)
        def _():
            pool_sum(c - 1)

        return carry

    def pool_sum(c):
        arrived(brecv.at[c], "bk_p", c)
        bsum[c] = (bsum[c].astype(F32) + brecv[c].astype(F32)).astype(BF16)
        for h in range(2):
            relay_copy(h, c).start()
        partial_copy(1, 0, c).start()
        partial_copy(2, 1, c).start()

    def relay_sums(c):
        for e in (2, 1):
            relayed(e, c).start()

    lax.fori_loop(0, n_c, back_chunk, 0)
    pool_sum(n_c - 1)
    @pl.when(mine)
    def _():
        for d in range(1, n_ka):
            region = xtbuf.at[:, :, ka_rows(k_from(d))]
            arrived(region, "xt_ka", d)
            remote(region, region, "xt_fw", d, partner).start()

    early = min(3, n_c)
    for c in range(early):
        relay_sums(c)

    for d in range(1, n_pb):
        region = gp.at[b_from(d), :, q_cols(p)]
        arrived(region, "dq_z", d)
        send(region, region, "dq_p", d, partner)
    for d in range(1, n_pb):
        region = gp.at[b_from(d), half_rows(p), pl.ds(kv_at, 2 * hd)]
        arrived(region, "gk_z", d)
        send(region, region, "gk_p", d, partner)
    for d in range(1, n_pb):
        arrived(modbuf.at[b_from(d)], "mod", d)
    for d in range(1, n_pb):
        arrived(gp.at[b_from(d), :, q_cols(other)], "dq_p", d)
        arrived(gp.at[b_from(d), half_rows(other), pl.ds(kv_at, 2 * hd)], "gk_p", d)
        source = b_from(d)
        mgp[source] = jnp.where(own_mask(source), gp[source].astype(F32), 0.0).astype(BF16)

    @pl.when(jnp.logical_not(mine))
    def _():
        for d in range(n_ka):
            arrived(xtbuf.at[:, :, ka_rows(k_from(d))], "xt_fw", d)

    tiles = max(t for t in range(1, 7) if slice_rows % (16 * t) == 0)
    w_tile = slice_rows // tiles

    def weight_rows(t):
        at = pl.ds(pl.multiple_of(t * w_tile, 16), w_tile)
        acc = jnp.dot(xtbuf[0, at, :], mgp[0], preferred_element_type=F32)
        for i in range(1, n_pb):
            acc += jnp.dot(xtbuf[i, at, :], mgp[i], preferred_element_type=F32)
        wout[at, :] = acc

    def weight_and_relay(t, carry):
        weight_rows(t)

        @pl.when(t + early < n_c)
        def _():
            relay_sums(t + early)

        return carry

    lax.fori_loop(0, tiles, weight_and_relay, 0)
    for c in range(early + tiles, n_c):
        relay_sums(c)
    store = pltpu.make_async_copy(wout, out_weight.at[0], store_sem)
    store.start()

    for c in range(n_c):
        acc = bsum[c, ka_rows(k), :].astype(F32)
        for e in (1, 2):
            for h in range(2):
                arrived(kar.at[e - 1, c, pl.ds(h * part, part)], "kar", (2 * (e - 1) + h) * n_c + c)
            acc += kar[e - 1, c].astype(F32)
        out_tok[:, c * chunk : (c + 1) * chunk] = acc.astype(BF16)

    store.wait()
    for copy in sends:
        copy.wait_send()
    for d in range(1, n_pb):
        target = lax.rem(b + d, n_pb)

        @pl.when(lax.div(target, hp) == p)
        def _(d=d, target=target):
            remote(xt.at[xt_part(target)], xtbuf.at[b, :, ka_rows(k)], "xt_z", d, pb_dev(d)).wait_send()

    @pl.when(mine)
    def _():
        region = xtbuf.at[:, :, ka_rows(k)]
        for d in range(1, n_ka):
            remote(region, region, "xt_ka", d, ka_dev(d)).wait_send()
        for d in range(n_ka):
            region = xtbuf.at[:, :, ka_rows(k_from(d))]
            remote(region, region, "xt_fw", d, partner).wait_send()

    def sent(c, carry):
        remote(bsend.at[c], brecv.at[c], "bk_p", c, partner).wait_send()
        for h in range(2):
            relay_copy(h, c).wait_send()
            for e in (1, 2):
                partial_copy(e, h, c).wait_send()
        return carry

    lax.fori_loop(0, n_c, sent, 0)


def hand_over(tok_from, weight_from, tok_to, weight_to, tok_mid, weight_mid, in_sems, out_sems):
    count = in_sems.shape[0]
    pieces = []
    for source, middle, target, first, parts in (
        (weight_from.at[0], weight_mid, weight_to.at[0], 0, count - 1),
        (tok_from, tok_mid, tok_to, count - 1, 1),
    ):
        if source.shape[0] % (16 * parts):
            parts = 1
        rows = source.shape[0] // parts
        for i in range(parts):
            at = pl.ds(i * rows, rows)
            pieces.append(
                (
                    pltpu.make_async_copy(source.at[at], middle.at[at], in_sems.at[first + i]),
                    pltpu.make_async_copy(middle.at[at], target.at[at], out_sems.at[first + i]),
                )
            )
    for read, _ in pieces:
        read.start()
    for read, write in pieces:
        read.wait()
        write.start()
    for _, write in pieces:
        write.wait()


def shards(tokens, modality, proj_weight, out_grad):
    n_pool, n_pb, n_ka = (lax.axis_size(name) for name in ("pool", "pb", "ka"))
    rows, half = tokens.shape
    group = proj_weight.shape[2]
    width = proj_weight.shape[1]
    q_rows, hd = out_grad.shape[1:]
    keys = n_pb * q_rows
    slice_rows = width // n_pb
    chunk = divisor(half, 128, 512)
    n_c = half // chunk
    vmem, scratch_bytes = [], 0
    shapes = [
        ((2, q_rows, half), BF16), ((width, group), BF16), ((n_pb, slice_rows, q_rows), BF16),
        ((n_pb, q_rows, hd), BF16), ((q_rows, group), BF16), ((q_rows, group), BF16),
        ((q_rows, hd), BF16), ((n_pb, n_ka, 2, rows // 2, 2 * hd), BF16), ((hd, keys), BF16),
        ((n_pb, q_rows, q_rows), BF16), ((n_pb, q_rows, q_rows), BF16), ((n_pb, 2, q_rows // 2, 2 * hd), BF16),
        ((n_pb, q_rows // 2, 2 * hd), BF16), ((n_pb, q_rows // 2, 2 * hd), BF16),
        ((n_pb, q_rows // 2, 2 * hd), BF16), ((n_pb, q_rows, group), BF16),
        ((n_pb, q_rows, group), BF16), ((n_c, q_rows, chunk), BF16), ((n_c, q_rows, chunk), BF16),
        ((n_c, q_rows, chunk), BF16), ((2, n_c, rows, chunk), BF16),
        ((2, n_c, rows // 2, chunk), BF16), ((half, rows), BF16), ((slice_rows, group), F32),
    ]
    for shape, kind in shapes:
        vmem.append(pltpu.VMEM(shape, kind))
        scratch_bytes += math.prod(shape) * jnp.dtype(kind).itemsize
    scratch_bytes += 5 * keys * min(256, q_rows) * 4
    if scratch_bytes > 58 * 2**20 or n_pool != 2 or n_pb % 2 or n_ka != 4:
        return plain_shards(tokens, modality, proj_weight, out_grad)
    offsets, count = {}, 0
    for name, size in (
        ("tok_ka", 2 * n_ka), ("tok_fw", 2 * n_ka), ("mod", n_pb), ("xt_z", n_pb), ("xt_ka", n_ka),
        ("xt_fw", n_ka), ("pj", n_ka), ("kv_z", n_pb * n_ka), ("kv_fw", n_pb * n_ka), ("dk_p", n_pb), ("dk_z", n_pb),
        ("dq_p", n_pb), ("dq_z", n_pb), ("gk_p", n_pb), ("gk_z", n_pb), ("bk_p", n_c),
        ("kar", 4 * n_c), ("rel", 2 * n_c),
    ):
        offsets[name] = count
        count += size
    dims = (n_pb, n_ka, rows, half, group, hd, q_rows, offsets)
    in_vmem = pl.BlockSpec(memory_space=pltpu.VMEM)
    kinds = jnp.broadcast_to(modality.astype(BF16)[:, None], (q_rows, hd))
    made = pl.pallas_call(
        functools.partial(fused, dims),
        out_shape=(
            jax.ShapeDtypeStruct((rows, half), BF16),
            jax.ShapeDtypeStruct((1, slice_rows, group), F32),
        ),
        in_specs=[in_vmem, in_vmem, pl.BlockSpec(memory_space=pl.ANY), in_vmem],
        out_specs=(in_vmem, pl.BlockSpec(memory_space=pl.ANY)),
        scratch_shapes=vmem
        + [
            pltpu.SemaphoreType.DMA,
            pltpu.SemaphoreType.DMA,
            pltpu.SemaphoreType.DMA((count,)),
            pltpu.SemaphoreType.DMA((count,)),
        ],
        compiler_params=pltpu.CompilerParams(
            collective_id=0, has_side_effects=True, vmem_limit_bytes=62 * 2**20
        ),
    )(tokens, kinds, proj_weight, out_grad)
    any_space = pl.BlockSpec(memory_space=pl.ANY)
    return pl.pallas_call(
        hand_over,
        out_shape=tuple(jax.ShapeDtypeStruct(x.shape, x.dtype) for x in made),
        in_specs=[any_space, any_space],
        out_specs=(any_space, any_space),
        scratch_shapes=[
            pltpu.VMEM(made[0].shape, made[0].dtype),
            pltpu.VMEM(made[1].shape[1:], made[1].dtype),
            pltpu.SemaphoreType.DMA((5,)),
            pltpu.SemaphoreType.DMA((5,)),
        ],
        compiler_params=pltpu.CompilerParams(vmem_limit_bytes=62 * 2**20),
    )(*made)


def solution(mesh):
    return jax.shard_map(
        shards,
        mesh=mesh,
        in_specs=(P(("pb", "ka"), "pool"), P("pb"), P("pool", None, "ka"), P("pool", "pb", "ka")),
        out_specs=(P(("pb", "ka"), "pool"), P("pool", "pb", "ka")),
        check_vma=False,
    )
```
